32 devices in a mesh: dom: 8 (over z, x), grp: 4 (over y, core).
Axes of the slice: x: 2, y: 2, z: 4, core: 2. Of those that a mesh axis runs over, the one named last changes fastest.
Arguments:
- node_latents: bfloat16 [4, 2048, 256], P('grp', 'dom'), may hold values from -6 to 6
- ghost_latents: bfloat16 [4, 512, 256], P('grp', 'dom'), may hold values from -6 to 6
- edge_latents: bfloat16 [4, 4096, 256], P('grp', 'dom'), may hold values from -6 to 6
- node_cotangent: bfloat16 [4, 2048, 256], P('grp', 'dom'), may hold values from -6 to 6
- edge_cotangent: bfloat16 [4, 4096, 256], P('grp', 'dom'), may hold values from -6 to 6
- senders: int32 [4, 4096], P('grp', 'dom'), may hold values from 0 to 319, as said below
- receivers: int32 [4, 4096], P('grp', 'dom'), may hold values from 0 to 255
- halo_counts: int32 [4, 32], P('grp', 'dom'), may hold values from 0 to 16, as said below
- recv_index: int32 [4, 32, 16], P('grp', 'dom'), may hold values from 0 to 255
- edge_w1: bfloat16 [768, 256], replicated, may hold values from -0.21875 to 0.21875
- edge_w2: bfloat16 [256, 256], replicated, may hold values from -0.375 to 0.375
- edge_w3: bfloat16 [256, 256], replicated, may hold values from -0.375 to 0.375
- edge_gain: float32 [256], replicated, may hold values from 0.5 to 1.5
- node_w1: bfloat16 [512, 256], replicated, may hold values from -0.25 to 0.25
- node_w2: bfloat16 [256, 256], replicated, may hold values from -0.375 to 0.375
- node_w3: bfloat16 [256, 256], replicated, may hold values from -0.375 to 0.375
- node_gain: float32 [256], replicated, may hold values from 0.5 to 1.5
Outputs:
- grad_node: bfloat16 [4, 2048, 256], P('grp', 'dom')
- grad_edge: bfloat16 [4, 4096, 256], P('grp', 'dom')
- grad_edge_w1: float32 [768, 256], P('grp')
- grad_edge_w2: float32 [256, 256], P('grp')
- grad_edge_w3: float32 [256, 256], P('grp')
- grad_edge_gain: float32 [256], P('grp')
- grad_node_w1: float32 [512, 256], P('grp')
- grad_node_w2: float32 [256, 256], P('grp')
- grad_node_w3: float32 [256, 256], P('grp')
- grad_node_gain: float32 [256], P('grp')
The draws below stay inside these ranges and needn't reach their ends.
Inputs may be any that keep to these rules, and one draw needn't show every extreme that they name: Ghost senders name only live slots, s below halo_counts of their direction; every other sender is an owned node. `halo_counts`: directions that point past the group's ends hold 0; every partition has a direction holding exactly 16.
All inputs are finite; a program needn't handle non-finite values.
Results may differ from the reference program's by a relative error of at most 0.013.
Values may be sent and summed in bfloat16 or wider, within the bound.
A program may use at most 64 MiB of HBM per device.

```python
import math
import jax
import jax.numpy as jnp
from jax import lax

LATENT = 256
NODE_DEV = 256
E_DEV = 512
SLOTS = 16
GHOST = 64
GROUPS = 4
NODES = 2048
EDGES = 4096
GHOSTS = 512
N_DOM = 8


def slot_counts(key):
    key = jax.random.fold_in(key, 11)
    key_count, key_coin = jax.random.split(key)
    counts = jax.random.randint(key_count, (GROUPS, N_DOM, 4), SLOTS // 2, SLOTS + 1)
    domain = jnp.arange(N_DOM, dtype=jnp.int32)[None, :, None]
    offsets = jnp.array([-2, -1, 1, 2], jnp.int32)[None, None, :]
    in_range = (domain + offsets >= 0) & (domain + offsets < N_DOM)
    coin_flip = jax.random.randint(key_coin, (GROUPS, N_DOM, 1), 1, 3)
    forced = jnp.where(domain == 0, 3, jnp.where(domain == N_DOM - 1, 1, coin_flip))
    direction = jnp.arange(4, dtype=jnp.int32)[None, None, :]
    counts = jnp.where(direction == forced, SLOTS, counts)
    return (jnp.where(in_range, counts, 0).astype(jnp.int32), forced)


def draw_halo_counts(key, part):
    counts, forced = slot_counts(key)
    return counts.reshape(GROUPS, N_DOM * 4)


def draw_senders(key, part):
    counts, forced = slot_counts(key)
    key = jax.random.fold_in(key, 5)
    chosen = jax.random.randint(key, (GROUPS, N_DOM, E_DEV), 0, NODE_DEV + GHOST)
    ghost_slot = chosen - NODE_DEV
    direction = jnp.clip(ghost_slot // SLOTS, 0, 3)
    slot_limit = jnp.take_along_axis(counts, direction, axis=2)
    is_live = (ghost_slot < 0) | (ghost_slot % SLOTS < slot_limit)
    chosen = jnp.where(is_live, chosen, chosen % NODE_DEV)
    position = jnp.arange(E_DEV, dtype=jnp.int32)[None, None, :]
    last_slot = NODE_DEV + forced * SLOTS + SLOTS - 1
    chosen = jnp.where(position == 0, last_slot, chosen)
    chosen = jnp.where(position == 1, 0, chosen)
    return chosen.reshape(GROUPS, EDGES).astype(jnp.int32)


def touch_ends(drawn, rng, smallest, largest):
    index_at = [jax.random.randint(jax.random.fold_in(rng, axis), (), 0, length) for axis, length in enumerate(drawn.shape)]
    longest = drawn.shape.index(max(drawn.shape))
    next_to = index_at[:longest] + [(index_at[longest] + 1) % drawn.shape[longest]] + index_at[longest + 1:]
    return drawn.at[tuple(index_at)].set(smallest).at[tuple(next_to)].set(largest)


def shard_levels(rng, dims, shards, least, top_value):
    loudness = 1.0
    for dim, blocks in shards:
        steps = jax.random.uniform(jax.random.fold_in(jax.random.fold_in(rng, 6), dim), (blocks,), jnp.float32, least / len(shards), top_value / len(shards))
        loudness = loudness * jnp.repeat(jnp.exp(steps), dims[dim] // blocks).reshape((-1,) + (1,) * (len(dims) - 1 - dim))
    return loudness


def noise(own_key, shape, width, bound, cuts=(), kind=jnp.bfloat16):
    values = width * jax.random.normal(own_key, shape, jnp.float32)
    if cuts:
        values = values * shard_levels(own_key, shape, cuts, -0.22, 0.18)
    return jnp.clip(values, -bound, bound).astype(kind)


def setup_inputs(seed: int = 0) -> dict:
    key_list = jax.random.split(jax.random.key(seed), 18)
    return {
        "node_latents": noise(key_list[0], (GROUPS, NODES, LATENT), 1.0, 6.0, ((0, 4), (1, 8))),
        "ghost_latents": noise(key_list[1], (GROUPS, GHOSTS, LATENT), 1.0, 6.0, ((0, 4), (1, 8))),
        "edge_latents": noise(key_list[2], (GROUPS, EDGES, LATENT), 1.0, 6.0, ((0, 4), (1, 8))),
        "node_cotangent": noise(key_list[3], (GROUPS, NODES, LATENT), 1.0, 6.0, ((0, 4), (1, 8))),
        "edge_cotangent": noise(key_list[4], (GROUPS, EDGES, LATENT), 1.0, 6.0, ((0, 4), (1, 8))),
        "senders": draw_senders(jax.random.fold_in(key_list[17], 71), 0),
        "receivers": touch_ends(jax.random.randint(key_list[6], (GROUPS, EDGES), 0, NODE_DEV), jax.random.fold_in(key_list[6], 1), 0, NODE_DEV - 1).astype(jnp.int32),
        "halo_counts": draw_halo_counts(jax.random.fold_in(key_list[17], 71), 0),
        "recv_index": touch_ends(jax.random.randint(key_list[8], (GROUPS, N_DOM * 4, SLOTS), 0, NODE_DEV), jax.random.fold_in(key_list[8], 1), 0, NODE_DEV - 1).astype(jnp.int32),
        "edge_w1": noise(key_list[9], (3 * LATENT, LATENT), (3 * LATENT) ** -0.5, 0.21875),
        "edge_w2": noise(key_list[10], (LATENT, LATENT), LATENT ** -0.5, 0.375),
        "edge_w3": noise(key_list[11], (LATENT, LATENT), LATENT ** -0.5, 0.375),
        "edge_gain": jnp.clip(jax.random.uniform(key_list[12], (LATENT,), jnp.float32, 0.5, 1.5), 0.5, 1.5),
        "node_w1": noise(key_list[13], (2 * LATENT, LATENT), (2 * LATENT) ** -0.5, 0.25),
        "node_w2": noise(key_list[14], (LATENT, LATENT), LATENT ** -0.5, 0.375),
        "node_w3": noise(key_list[15], (LATENT, LATENT), LATENT ** -0.5, 0.375),
        "node_gain": jnp.clip(jax.random.uniform(key_list[16], (LATENT,), jnp.float32, 0.5, 1.5), 0.5, 1.5),
    }


EPS = 1e-05
OFFSETS = (-2, -1, 1, 2)

def matmul(left, right):
    return jnp.dot(left, right, preferred_element_type=jnp.float32)

def over_rows(left, right):
    return lax.dot_general(left, right, (((0,), (0,)), ((), ())), preferred_element_type=jnp.float32)

def against(left, weight):
    return lax.dot_general(left, weight, (((1,), (1,)), ((), ())), preferred_element_type=jnp.float32)

def silu_slope(value):
    sigma = jax.nn.sigmoid(value)
    return sigma * (1.0 + value * (1.0 - sigma))

def norm_parts(value):
    centre = value - lax.optimization_barrier(jnp.mean(value, axis=-1, keepdims=True))
    scale = lax.rsqrt(lax.optimization_barrier(jnp.mean(centre * centre, axis=-1, keepdims=True)) + EPS)
    return (centre * scale, scale)

def norm_back(upstream, normed, scale):
    return scale * (upstream - lax.optimization_barrier(jnp.mean(upstream, axis=-1, keepdims=True)) - normed * lax.optimization_barrier(jnp.mean(upstream * normed, axis=-1, keepdims=True)))

def mlp_forward(inputs, first_w, second_w, third_w, gain):
    pre_one = matmul(inputs, first_w)
    act_one = jax.nn.silu(pre_one).astype(jnp.bfloat16)
    pre_two = matmul(act_one, second_w)
    act_two = jax.nn.silu(pre_two).astype(jnp.bfloat16)
    normed, scale = norm_parts(matmul(act_two, third_w))
    return (normed * gain, (pre_one, act_one, pre_two, act_two, normed, scale))

def mlp_backward(inputs, first_w, second_w, third_w, gain, saved, upstream):
    pre_one, act_one, pre_two, act_two, normed, scale = saved
    grad_gain = lax.optimization_barrier(jnp.sum(upstream * normed, axis=0))
    delta_out = norm_back(upstream * gain, normed, scale).astype(jnp.bfloat16)
    grad_third = over_rows(act_two, delta_out)
    delta_two = (against(delta_out, third_w) * silu_slope(pre_two)).astype(jnp.bfloat16)
    grad_second = over_rows(act_one, delta_two)
    delta_one = (against(delta_two, second_w) * silu_slope(pre_one)).astype(jnp.bfloat16)
    grad_first = over_rows(inputs, delta_one)
    return (against(delta_one, first_w), (grad_first, grad_second, grad_third, grad_gain))

def local_pass(node_lat, ghost_lat, edge_lat, node_cot, edge_cot, sender_ids, receiver_ids, counts, weights):
    edge_one, edge_two, edge_three, edge_g, node_one, node_two, node_three, node_g = weights
    node_count = node_lat.shape[0]
    ghost_count = ghost_lat.shape[0]
    slot_count = ghost_count // 4
    latent = node_lat.shape[1]
    node_table = jnp.concatenate([node_lat, ghost_lat], axis=0)
    send_hot = (sender_ids[:, None] == lax.iota(jnp.int32, node_count + ghost_count)[None, :]).astype(jnp.bfloat16)
    recv_hot = (receiver_ids[:, None] == lax.iota(jnp.int32, node_count)[None, :]).astype(jnp.bfloat16)
    sender_lat = matmul(send_hot, node_table).astype(jnp.bfloat16)
    receiver_lat = matmul(recv_hot, node_lat).astype(jnp.bfloat16)
    edge_in = jnp.concatenate([edge_lat, sender_lat, receiver_lat], axis=1)
    message, edge_saved = mlp_forward(edge_in, edge_one, edge_two, edge_three, edge_g)
    updated = (edge_lat.astype(jnp.float32) + message).astype(jnp.bfloat16)
    summed = over_rows(recv_hot, updated).astype(jnp.bfloat16)
    node_in = jnp.concatenate([node_lat, summed], axis=1)
    unused_out, node_saved = mlp_forward(node_in, node_one, node_two, node_three, node_g)
    node_up = node_cot.astype(jnp.float32)
    node_grad_in, node_terms = mlp_backward(node_in, node_one, node_two, node_three, node_g, node_saved, node_up)
    back_summed = node_grad_in[:, latent:].astype(jnp.bfloat16)
    edge_up = edge_cot.astype(jnp.float32) + matmul(recv_hot, back_summed)
    edge_grad_in, edge_terms = mlp_backward(edge_in, edge_one, edge_two, edge_three, edge_g, edge_saved, edge_up)
    grad_edge = (edge_up + edge_grad_in[:, :latent]).astype(jnp.bfloat16)
    to_sender = edge_grad_in[:, latent:2 * latent].astype(jnp.bfloat16)
    to_receiver = edge_grad_in[:, 2 * latent:].astype(jnp.bfloat16)
    to_table = over_rows(send_hot, to_sender)
    node_total = node_up + node_grad_in[:, :latent] + over_rows(recv_hot, to_receiver) + to_table[:node_count]
    ghost_grad = to_table[node_count:].reshape(4, slot_count, latent)
    is_live = lax.iota(jnp.int32, slot_count)[None, :] < counts[:, None]
    ghost_grad = jnp.where(is_live[:, :, None], ghost_grad, 0.0).astype(jnp.bfloat16)
    return (grad_edge, node_total, ghost_grad, edge_terms + node_terms)

def add_rows(node_total, targets, values):
    return node_total.at[targets].add(values)

def reference(node_latents, ghost_latents, edge_latents, node_cotangent, edge_cotangent, senders, receivers, halo_counts, recv_index, edge_w1, edge_w2, edge_w3, edge_gain, node_w1, node_w2, node_w3, node_gain):
    weights = (edge_w1, edge_w2, edge_w3, edge_gain, node_w1, node_w2, node_w3, node_gain)
    devices = GROUPS * N_DOM
    pieces = (node_latents.reshape(devices, NODE_DEV, LATENT), ghost_latents.reshape(devices, GHOST, LATENT), edge_latents.reshape(devices, E_DEV, LATENT), node_cotangent.reshape(devices, NODE_DEV, LATENT), edge_cotangent.reshape(devices, E_DEV, LATENT), senders.reshape(devices, E_DEV), receivers.reshape(devices, E_DEV), halo_counts.reshape(devices, 4))

    def device_step(running, piece):
        grad_edge, node_total, ghost_grad, grad_terms = local_pass(*piece, weights)
        rounded = tuple((lax.optimization_barrier(term.astype(jnp.bfloat16)).astype(jnp.float32) for term in grad_terms))
        running = tuple((left + right for left, right in zip(running, rounded)))
        return (running, (grad_edge, node_total, ghost_grad))
    start = tuple((jnp.zeros(weight.shape, jnp.float32) for weight in weights))
    running, (grad_edge, node_total, ghost_grad) = lax.scan(device_step, start, pieces)
    ghost_grad = ghost_grad.reshape(GROUPS, N_DOM, 4, SLOTS, LATENT)
    padded = jnp.pad(ghost_grad, ((0, 0), (2, 2), (0, 0), (0, 0), (0, 0)))
    arrived = jnp.stack([padded[:, 2 - offset:2 - offset + N_DOM, direction] for direction, offset in enumerate(OFFSETS)], axis=2)
    node_total = jax.vmap(add_rows)(node_total, recv_index.reshape(devices, 4 * SLOTS), arrived.reshape(devices, 4 * SLOTS, LATENT).astype(jnp.float32))
    grad_node = node_total.astype(jnp.bfloat16).reshape(GROUPS, NODES, LATENT)
    edge_scale = 1.0 / math.sqrt(GROUPS * EDGES)
    node_scale = 1.0 / math.sqrt(GROUPS * NODES)
    return (grad_node, grad_edge.reshape(GROUPS, EDGES, LATENT), running[0] * edge_scale, running[1] * edge_scale, running[2] * edge_scale, running[3] * edge_scale, running[4] * node_scale, running[5] * node_scale, running[6] * node_scale, running[7] * node_scale)
```

```python
import functools
import math

import jax
import jax.numpy as jnp
from jax import lax
from jax.experimental import pallas as pl
from jax.experimental.pallas import tpu as pltpu
from jax.sharding import PartitionSpec as P

EPS = 1e-05
OFFSETS = (-2, -1, 1, 2)


def from_behind(block, axis, distance):
    devices = range(lax.axis_size(axis))
    route = [(i - distance, i) for i in devices if i - distance in devices]
    return lax.ppermute(block, axis, route)


def matmul(left, right):
    return jnp.dot(left, right, preferred_element_type=jnp.float32)


def over_rows(left, right):
    return lax.dot_general(
        left, right, (((0,), (0,)), ((), ())), preferred_element_type=jnp.float32
    )


def against(left, weight):
    return lax.dot_general(
        left, weight, (((1,), (1,)), ((), ())), preferred_element_type=jnp.float32
    )


def silu_slope(value):
    sigma = jax.nn.sigmoid(value)
    return sigma * (1.0 + value * (1.0 - sigma))


def norm_parts(value):
    centre = value - jnp.mean(value, axis=-1, keepdims=True)
    scale = lax.rsqrt(jnp.mean(centre * centre, axis=-1, keepdims=True) + EPS)
    return (centre * scale, scale)


def norm_back(upstream, normed, scale):
    return scale * (
        upstream
        - jnp.mean(upstream, axis=-1, keepdims=True)
        - normed * jnp.mean(upstream * normed, axis=-1, keepdims=True)
    )


def mlp_forward(inputs, first_w, second_w, third_w, gain):
    pre_one = matmul(inputs, first_w)
    act_one = jax.nn.silu(pre_one).astype(jnp.bfloat16)
    pre_two = matmul(act_one, second_w)
    act_two = jax.nn.silu(pre_two).astype(jnp.bfloat16)
    normed, scale = norm_parts(matmul(act_two, third_w))
    return (normed * gain, (pre_one, act_one, pre_two, act_two, normed, scale))


def mlp_backward(inputs, first_w, second_w, third_w, gain, saved, upstream):
    pre_one, act_one, pre_two, act_two, normed, scale = saved
    grad_gain = jnp.sum(upstream * normed, axis=0)
    delta_out = norm_back(upstream * gain, normed, scale).astype(jnp.bfloat16)
    grad_third = over_rows(act_two, delta_out)
    delta_two = (against(delta_out, third_w) * silu_slope(pre_two)).astype(jnp.bfloat16)
    grad_second = over_rows(act_one, delta_two)
    delta_one = (against(delta_two, second_w) * silu_slope(pre_one)).astype(jnp.bfloat16)
    grad_first = over_rows(inputs, delta_one)
    return (against(delta_one, first_w), (grad_first, grad_second, grad_third, grad_gain))


def local_pass(
    node_lat, ghost_lat, edge_lat, node_cot, edge_cot, sender_ids, receiver_ids, counts, weights
):
    edge_one, edge_two, edge_three, edge_g, node_one, node_two, node_three, node_g = weights
    node_count = node_lat.shape[0]
    ghost_count = ghost_lat.shape[0]
    slot_count = ghost_count // 4
    latent = node_lat.shape[1]
    node_table = jnp.concatenate([node_lat, ghost_lat], axis=0)
    send_hot = (
        sender_ids[:, None] == lax.iota(jnp.int32, node_count + ghost_count)[None, :]
    ).astype(jnp.bfloat16)
    recv_hot = (receiver_ids[:, None] == lax.iota(jnp.int32, node_count)[None, :]).astype(
        jnp.bfloat16
    )
    sender_lat = matmul(send_hot, node_table).astype(jnp.bfloat16)
    receiver_lat = matmul(recv_hot, node_lat).astype(jnp.bfloat16)
    edge_in = jnp.concatenate([edge_lat, sender_lat, receiver_lat], axis=1)
    message, edge_saved = mlp_forward(edge_in, edge_one, edge_two, edge_three, edge_g)
    updated = (edge_lat.astype(jnp.float32) + message).astype(jnp.bfloat16)
    summed = over_rows(recv_hot, updated).astype(jnp.bfloat16)
    node_in = jnp.concatenate([node_lat, summed], axis=1)
    unused_out, node_saved = mlp_forward(node_in, node_one, node_two, node_three, node_g)
    node_up = node_cot.astype(jnp.float32)
    node_grad_in, node_terms = mlp_backward(
        node_in, node_one, node_two, node_three, node_g, node_saved, node_up
    )
    back_summed = node_grad_in[:, latent:].astype(jnp.bfloat16)
    edge_up = edge_cot.astype(jnp.float32) + matmul(recv_hot, back_summed)
    edge_grad_in, edge_terms = mlp_backward(
        edge_in, edge_one, edge_two, edge_three, edge_g, edge_saved, edge_up
    )
    grad_edge = (edge_up + edge_grad_in[:, :latent]).astype(jnp.bfloat16)
    to_sender = edge_grad_in[:, latent : 2 * latent].astype(jnp.bfloat16)
    to_receiver = edge_grad_in[:, 2 * latent :].astype(jnp.bfloat16)
    to_table = over_rows(send_hot, to_sender)
    node_total = (
        node_up
        + node_grad_in[:, :latent]
        + over_rows(recv_hot, to_receiver)
        + to_table[:node_count]
    )
    ghost_grad = to_table[node_count:].reshape(4, slot_count, latent)
    is_live = lax.iota(jnp.int32, slot_count)[None, :] < counts[:, None]
    ghost_grad = jnp.where(is_live[:, :, None], ghost_grad, 0.0).astype(jnp.bfloat16)
    return (grad_edge, node_total, ghost_grad, edge_terms + node_terms)


def per_device(
    node_latents,
    ghost_latents,
    edge_latents,
    node_cotangent,
    edge_cotangent,
    senders,
    receivers,
    halo_counts,
    recv_index,
    edge_w1,
    edge_w2,
    edge_w3,
    edge_gain,
    node_w1,
    node_w2,
    node_w3,
    node_gain,
):
    weights = (edge_w1, edge_w2, edge_w3, edge_gain, node_w1, node_w2, node_w3, node_gain)
    grad_edge, node_total, ghost_grad, grad_terms = local_pass(
        node_latents[0],
        ghost_latents[0],
        edge_latents[0],
        node_cotangent[0],
        edge_cotangent[0],
        senders[0],
        receivers[0],
        halo_counts[0],
        weights,
    )
    (
        edge_first,
        edge_second,
        edge_third,
        edge_gsum,
        node_first,
        node_second,
        node_third,
        node_gsum,
    ) = grad_terms
    domains = lax.axis_size("dom")
    groups = lax.axis_size("grp")
    reduced = (
        lax.psum_scatter(
            edge_first.astype(jnp.bfloat16), "grp", scatter_dimension=0, tiled=True
        ).astype(jnp.float32),
        lax.psum_scatter(
            edge_second.astype(jnp.bfloat16), "grp", scatter_dimension=0, tiled=True
        ).astype(jnp.float32),
        lax.psum_scatter(
            edge_third.astype(jnp.bfloat16), "grp", scatter_dimension=0, tiled=True
        ).astype(jnp.float32),
        lax.psum_scatter(
            edge_gsum.astype(jnp.bfloat16), "grp", scatter_dimension=0, tiled=True
        ).astype(jnp.float32),
        lax.psum_scatter(
            node_first.astype(jnp.bfloat16), "grp", scatter_dimension=0, tiled=True
        ).astype(jnp.float32),
        lax.psum_scatter(
            node_second.astype(jnp.bfloat16), "grp", scatter_dimension=0, tiled=True
        ).astype(jnp.float32),
        lax.psum_scatter(
            node_third.astype(jnp.bfloat16), "grp", scatter_dimension=0, tiled=True
        ).astype(jnp.float32),
        lax.psum_scatter(
            node_gsum.astype(jnp.bfloat16), "grp", scatter_dimension=0, tiled=True
        ).astype(jnp.float32),
    )
    reduced = lax.psum(
        (
            reduced[0],
            reduced[1],
            reduced[2],
            reduced[3],
            reduced[4],
            reduced[5],
            reduced[6],
            reduced[7],
        ),
        "dom",
    )
    arrivals = []
    for direction, offset in enumerate(OFFSETS):
        arrivals.append(from_behind(ghost_grad[direction], "dom", offset))
    arrived = jnp.stack(arrivals)
    node_count = node_total.shape[0]
    targets = recv_index[0].reshape(-1)
    owner_hot = (lax.iota(jnp.int32, node_count)[:, None] == targets[None, :]).astype(jnp.bfloat16)
    node_total = node_total + matmul(owner_hot, arrived.reshape(targets.shape[0], -1))
    grad_node = node_total.astype(jnp.bfloat16)[None]
    partitions = domains * groups
    edge_scale = 1.0 / math.sqrt(partitions * edge_latents.shape[1])
    node_scale = 1.0 / math.sqrt(partitions * node_latents.shape[1])
    return (
        grad_node,
        grad_edge[None],
        reduced[0] * edge_scale,
        reduced[1] * edge_scale,
        reduced[2] * edge_scale,
        reduced[3] * edge_scale,
        reduced[4] * node_scale,
        reduced[5] * node_scale,
        reduced[6] * node_scale,
        reduced[7] * node_scale,
    )


MESH = pl.DeviceIdType.MESH


def one_hot(mask):
    return jnp.where(mask, 1.0, 0.0).astype(jnp.bfloat16)


def hot_pair(ids, count):
    edges = ids.shape[1]
    column = jnp.transpose(jnp.broadcast_to(ids, (128, edges)))
    blocks = []
    for start in range(0, count, 128):
        width = min(128, count - start)
        lane = lax.broadcasted_iota(jnp.int32, (edges, width), 1) + start
        blocks.append(one_hot(column[:, :width] == lane))
    row = lax.broadcasted_iota(jnp.int32, (count, edges), 0)
    return blocks, one_hot(ids == row)


def wide(value):
    return value.astype(jnp.float32)


def narrow(value):
    return value.astype(jnp.bfloat16)


def activate(pre):
    sigma = jax.nn.sigmoid(pre)
    return narrow(pre * sigma), sigma * (1.0 + pre * (1.0 - sigma))


def fused_kernel(
    plan,
    node_lat,
    ghost_lat,
    edge_lat,
    node_cot,
    edge_cot,
    senders,
    receivers,
    counts,
    recv_index,
    ew1,
    ew2,
    ew3,
    egain,
    nw1,
    nw2,
    nw3,
    ngain,
    grad_node,
    grad_edge,
    out_e1,
    out_e2,
    out_e3,
    out_eg,
    out_n1,
    out_n2,
    out_n3,
    out_ng,
    terms_n,
    terms_b,
    terms_c,
    core_n,
    core_b,
    core_c,
    half_n,
    half_b,
    half_c,
    keep_n,
    keep_b,
    keep_c,
    side_n,
    side_b,
    side_c,
    part_n,
    part_b,
    part_c,
    gath_n,
    gath_b,
    gath_c,
    fin_n,
    fin_b,
    fin_c,
    ghost_out,
    ghost_in,
    send_sem,
    recv_sem,
):
    domains, edge_scale, node_scale = plan
    latent = node_lat.shape[1]
    owned = node_lat.shape[0]
    ghosts = ghost_lat.shape[0]
    slots = ghosts // 4
    blocks = domains // 2
    half = latent // 2
    dom = lax.axis_index("dom")
    grp = lax.axis_index("grp")
    core = lax.rem(grp, 2)
    pair = lax.div(grp, 2)
    other_core = 2 * pair + 1 - core
    other_pair = 2 * (1 - pair) + core
    per_chunk = 2 + 2 * (domains - 1)

    def ahead(step):
        return lax.rem(dom + step + domains, domains)

    barrier = pltpu.get_barrier_semaphore()
    pl.semaphore_signal(barrier, inc=1, device_id={"grp": other_core}, device_id_type=MESH)
    pl.semaphore_signal(barrier, inc=1, device_id={"grp": other_pair}, device_id_type=MESH)
    for step in range(1, domains):
        pl.semaphore_signal(barrier, inc=1, device_id={"dom": ahead(step)}, device_id_type=MESH)

    def remote(src, dst, number, target):
        return pltpu.make_async_remote_copy(
            src_ref=src,
            dst_ref=dst,
            send_sem=send_sem.at[number],
            recv_sem=recv_sem.at[number],
            device_id=target,
            device_id_type=MESH,
        )

    chunks = (
        (terms_n, core_n, half_n, keep_n, side_n, part_n, gath_n, fin_n),
        (terms_b, core_b, half_b, keep_b, side_b, part_b, gath_b, fin_b),
        (terms_c, core_c, half_c, keep_c, side_c, part_c, gath_c, fin_c),
    )

    def put(number, matrices, tail=None):
        terms = chunks[number][0]
        for quarter in range(4):
            rows = []
            for matrix in matrices:
                share = matrix.shape[0] // 4
                rows.append(matrix[quarter * share : (quarter + 1) * share])
            rows = narrow(rows[0] if len(rows) == 1 else jnp.concatenate(rows, axis=0))
            size = rows.shape[0] // blocks
            for piece in range(domains):
                at = (piece // 2) * size
                lane = (piece % 2) * half
                terms[quarter % 2, quarter // 2, piece, 0:size] = rows[
                    at : at + size, lane : lane + half
                ]
                if tail is not None:
                    terms[quarter % 2, quarter // 2, piece, size : size + 16] = tail

    def over_core(number):
        terms, arrived = chunks[number][0:2]
        return remote(
            terms.at[1 - core], arrived, number * per_chunk, {"grp": other_core}
        )

    def over_pair(number):
        return remote(
            chunks[number][2], chunks[number][4], number * per_chunk + 1, {"grp": other_pair}
        )

    def over_dom(number):
        part, gath = chunks[number][5:7]
        return [
            remote(
                part.at[ahead(step)],
                gath.at[step],
                number * per_chunk + 1 + step,
                {"dom": ahead(step)},
            )
            for step in range(1, domains)
        ]

    def spread(number):
        fin = chunks[number][7]
        return [
            remote(
                fin.at[0],
                fin.at[step],
                number * per_chunk + domains + step,
                {"dom": ahead(step)},
            )
            for step in range(1, domains)
        ]

    def stage_pair(number):
        terms, arrived, send, keep = chunks[number][0:4]
        over_core(number).wait()
        send[...] = narrow(wide(terms[core, 1 - pair]) + wide(arrived[1 - pair]))
        over_pair(number).start()
        keep[...] = wide(terms[core, pair]) + wide(arrived[pair])

    def stage_dom(number):
        keep, side, part = chunks[number][3:6]
        over_pair(number).wait()
        part[...] = narrow(keep[...] + wide(side[...]))
        for copy in over_dom(number):
            copy.start()

    def stage_spread(number):
        part, gath, fin = chunks[number][5:8]
        for copy in over_dom(number):
            copy.wait()
        total = wide(part[dom])
        for step in range(1, domains):
            total = total + wide(gath[step])
        fin[0] = narrow(total[: fin.shape[1]])
        for copy in spread(number):
            copy.start()
        return total

    def stage_out(number, outs, scale):
        fin = chunks[number][7]
        for copy in spread(number):
            copy.wait()
        size = fin.shape[1]
        for piece in range(domains):
            value = wide(fin[lax.rem(dom - piece + domains, domains)]) * scale
            lane = (piece % 2) * half
            first = (piece // 2) * size
            base = 0
            for out in outs:
                low, high = max(first, base), min(first + size, base + out.shape[0])
                if low < high:
                    out[low - base : high - base, lane : lane + half] = value[
                        low - first : high - first
                    ]
                base += out.shape[0]

    sender_blocks, sender_rows = hot_pair(senders[...], owned + ghosts)
    receiver_blocks, receiver_rows = hot_pair(receivers[...], owned)
    receiver_hot = jnp.concatenate(receiver_blocks, axis=1)
    node_blocks = owned // 128
    sender_hot = jnp.concatenate(sender_blocks[:node_blocks], axis=1)
    ghost_hot = jnp.concatenate(sender_blocks[node_blocks:], axis=1)
    own_lat = node_lat[...]
    edge_in0 = edge_lat[...]
    edge_in1 = narrow(matmul(sender_hot, own_lat) + matmul(ghost_hot, ghost_lat[...]))
    edge_in2 = narrow(matmul(receiver_hot, own_lat))

    pre = (
        matmul(edge_in0, ew1[0:latent])
        + matmul(edge_in1, ew1[latent : 2 * latent])
        + matmul(edge_in2, ew1[2 * latent : 3 * latent])
    )
    e_act1, e_slope1 = activate(pre)
    e_act2, e_slope2 = activate(matmul(e_act1, ew2[...]))
    e_normed, e_norm = norm_parts(matmul(e_act2, ew3[...]))
    updated = narrow(wide(edge_in0) + e_normed * egain[...])
    summed = narrow(matmul(receiver_rows, updated))

    pre = matmul(own_lat, nw1[0:latent]) + matmul(summed, nw1[latent : 2 * latent])
    n_act1, n_slope1 = activate(pre)
    n_act2, n_slope2 = activate(matmul(n_act1, nw2[...]))
    n_normed, n_norm = norm_parts(matmul(n_act2, nw3[...]))
    node_up = wide(node_cot[...])
    n_gsum = jnp.sum(node_up * n_normed, axis=0, keepdims=True)
    q3 = narrow(norm_back(node_up * ngain[...], n_normed, n_norm))
    q2 = narrow(against(q3, nw3[...]) * n_slope2)
    q1 = narrow(against(q2, nw2[...]) * n_slope1)
    back_summed = narrow(against(q1, nw1[latent : 2 * latent]))
    put(
        0,
        (
            jnp.concatenate([over_rows(own_lat, q1), over_rows(summed, q1)], axis=0),
            over_rows(n_act1, q2),
            over_rows(n_act2, q3),
        ),
    )
    pl.semaphore_wait(barrier, domains + 1)
    over_core(0).start()

    node_part = node_up + against(q1, nw1[0:latent])
    edge_up = wide(edge_cot[...]) + matmul(receiver_hot, back_summed)
    e_gsum = jnp.sum(edge_up * e_normed, axis=0, keepdims=True)
    q3 = narrow(norm_back(edge_up * egain[...], e_normed, e_norm))
    stage_pair(0)
    q2 = narrow(against(q3, ew3[...]) * e_slope2)
    row = lax.broadcasted_iota(jnp.int32, (16, half), 0)
    tail = jnp.where(row == 0, e_gsum[:, :half], 0.0)
    tail = jnp.where(row == 1, e_gsum[:, half:], tail)
    tail = jnp.where(row == 2, n_gsum[:, :half], tail)
    tail = narrow(jnp.where(row == 3, n_gsum[:, half:], tail))
    put(1, (over_rows(e_act1, q2), over_rows(e_act2, q3)), tail)
    over_core(1).start()
    q1 = narrow(against(q2, ew2[...]) * e_slope1)
    put(
        2,
        (
            jnp.concatenate(
                [over_rows(edge_in0, q1), over_rows(edge_in1, q1), over_rows(edge_in2, q1)],
                axis=0,
            ),
        ),
    )
    over_core(2).start()
    stage_pair(1)
    stage_dom(0)

    to_sender = narrow(against(q1, ew1[latent : 2 * latent]))
    to_table = matmul(sender_rows, to_sender)
    slot = lax.broadcasted_iota(jnp.int32, (slots, latent), 0)
    halos = []
    for direction, offset in enumerate(OFFSETS):
        first = owned + direction * slots
        live = slot < counts[:, direction : direction + 1]
        ghost_out[direction] = narrow(jnp.where(live, to_table[first : first + slots], 0.0))
        halo = remote(
            ghost_out.at[direction],
            ghost_in.at[direction],
            3 * per_chunk + direction,
            {"dom": ahead(offset)},
        )
        halo.start()
        halos.append(halo)
    stage_pair(2)
    stage_dom(1)
    to_receiver = narrow(against(q1, ew1[2 * latent : 3 * latent]))
    node_part = node_part + to_table[:owned] + matmul(receiver_rows, to_receiver)
    stage_spread(0)
    grad_edge[...] = narrow(edge_up + against(q1, ew1[0:latent]))
    stage_dom(2)
    gains = stage_spread(1)
    gains = gains[gains.shape[0] - 16 :]
    quarter = latent // 4
    for out, first, scale in ((out_eg, 0, edge_scale), (out_ng, 2, node_scale)):
        line = jnp.where(pair == 0, gains[first : first + 1], gains[first + 1 : first + 2])
        out[...] = jnp.where(core == 0, line[:, :quarter], line[:, quarter:]) * scale
    for halo in halos:
        halo.wait()
    owner = lax.broadcasted_iota(jnp.int32, (owned, slots), 0)
    for direction in range(4):
        hot = one_hot(owner == recv_index[direction : direction + 1, :])
        node_part = node_part + matmul(hot, ghost_in[direction])
    grad_node[...] = narrow(node_part)
    stage_out(0, (out_n1, out_n2, out_n3), node_scale)
    stage_spread(2)
    stage_out(1, (out_e2, out_e3), edge_scale)
    stage_out(2, (out_e1,), edge_scale)


def fused_device(
    node_latents,
    ghost_latents,
    edge_latents,
    node_cotangent,
    edge_cotangent,
    senders,
    receivers,
    halo_counts,
    recv_index,
    edge_w1,
    edge_w2,
    edge_w3,
    edge_gain,
    node_w1,
    node_w2,
    node_w3,
    node_gain,
):
    domains = lax.axis_size("dom")
    groups = lax.axis_size("grp")
    nodes, latent = node_latents.shape[1:]
    edges = edge_latents.shape[1]
    slots = ghost_latents.shape[1] // 4
    partitions = domains * groups
    plan = (
        domains,
        1.0 / math.sqrt(partitions * edges),
        1.0 / math.sqrt(partitions * nodes),
    )
    half = latent // 2
    quarter = latent // 4
    blocks = domains // 2
    bulk = [
        node_w1.shape[0] // 4 + 2 * quarter,
        2 * quarter,
        edge_w1.shape[0] // 4,
    ]
    clean = [rows // blocks for rows in bulk]
    sizes = [clean[0], clean[1] + 16, clean[2]]

    def buffers(lead, kind, rows=sizes):
        return [pltpu.VMEM((*lead, size, half), kind) for size in rows]

    scratch = (
        buffers((2, 2, domains), jnp.bfloat16)
        + buffers((2, domains), jnp.bfloat16)
        + buffers((domains,), jnp.bfloat16)
        + buffers((domains,), jnp.float32)
        + buffers((domains,), jnp.bfloat16)
        + buffers((domains,), jnp.bfloat16)
        + buffers((domains,), jnp.bfloat16)
        + buffers((domains,), jnp.bfloat16, clean)
        + [
            pltpu.VMEM((4, slots, latent), jnp.bfloat16),
            pltpu.VMEM((4, slots, latent), jnp.bfloat16),
        ]
    )
    copies = 3 * (2 + 2 * (domains - 1)) + 4
    scratch += [pltpu.SemaphoreType.DMA((copies,)), pltpu.SemaphoreType.DMA((copies,))]
    vmem = pl.BlockSpec(memory_space=pltpu.VMEM)

    def grad(rows):
        return jax.ShapeDtypeStruct((rows, latent), jnp.float32)

    gain = jax.ShapeDtypeStruct((1, quarter), jnp.float32)
    outs = pl.pallas_call(
        functools.partial(fused_kernel, plan),
        out_shape=(
            jax.ShapeDtypeStruct((nodes, latent), jnp.bfloat16),
            jax.ShapeDtypeStruct((edges, latent), jnp.bfloat16),
            grad(edge_w1.shape[0] // 4),
            grad(quarter),
            grad(quarter),
            gain,
            grad(node_w1.shape[0] // 4),
            grad(quarter),
            grad(quarter),
            gain,
        ),
        in_specs=[vmem] * 17,
        out_specs=[vmem] * 10,
        scratch_shapes=scratch,
        compiler_params=pltpu.CompilerParams(
            collective_id=0, has_side_effects=True, vmem_limit_bytes=48 * 1024 * 1024
        ),
    )(
        node_latents[0],
        ghost_latents[0],
        edge_latents[0],
        node_cotangent[0],
        edge_cotangent[0],
        senders,
        receivers,
        halo_counts,
        recv_index[0],
        edge_w1,
        edge_w2,
        edge_w3,
        edge_gain[None],
        node_w1,
        node_w2,
        node_w3,
        node_gain[None],
    )
    outs = list(outs)
    outs[0] = outs[0][None]
    outs[1] = outs[1][None]
    outs[5] = outs[5][0]
    outs[9] = outs[9][0]
    return tuple(outs)


def solution(mesh):
    placed = (
        P("grp", "dom", None),
        P("grp", "dom", None),
        P("grp", "dom", None),
        P("grp", "dom", None),
        P("grp", "dom", None),
        P("grp", "dom"),
        P("grp", "dom"),
        P("grp", "dom"),
        P("grp", "dom", None),
        P(),
        P(),
        P(),
        P(),
        P(),
        P(),
        P(),
        P(),
    )
    domains, groups = mesh.shape["dom"], mesh.shape["grp"]
    fits = groups == 4 and domains == 8
    return jax.shard_map(
        fused_device if fits else per_device,
        mesh=mesh,
        in_specs=placed,
        out_specs=(
            P("grp", "dom", None),
            P("grp", "dom", None),
            P("grp", None),
            P("grp", None),
            P("grp", None),
            P("grp"),
            P("grp", None),
            P("grp", None),
            P("grp", None),
            P("grp"),
        ),
        check_vma=False,
    )
```

```python
import functools
import math

import jax
import jax.numpy as jnp
from jax import lax
from jax.experimental import pallas as pl
from jax.experimental.pallas import tpu as pltpu
from jax.sharding import PartitionSpec as P

EPS = 1e-05
OFFSETS = (-2, -1, 1, 2)


def from_behind(block, axis, distance):
    devices = range(lax.axis_size(axis))
    route = [(i - distance, i) for i in devices if i - distance in devices]
    return lax.ppermute(block, axis, route)


def matmul(left, right):
    return jnp.dot(left, right, preferred_element_type=jnp.float32)


def over_rows(left, right):
    return lax.dot_general(
        left, right, (((0,), (0,)), ((), ())), preferred_element_type=jnp.float32
    )


def against(left, weight):
    return lax.dot_general(
        left, weight, (((1,), (1,)), ((), ())), preferred_element_type=jnp.float32
    )


def silu_slope(value):
    sigma = jax.nn.sigmoid(value)
    return sigma * (1.0 + value * (1.0 - sigma))


def norm_parts(value):
    centre = value - jnp.mean(value, axis=-1, keepdims=True)
    scale = lax.rsqrt(jnp.mean(centre * centre, axis=-1, keepdims=True) + EPS)
    return (centre * scale, scale)


def norm_back(upstream, normed, scale):
    return scale * (
        upstream
        - jnp.mean(upstream, axis=-1, keepdims=True)
        - normed * jnp.mean(upstream * normed, axis=-1, keepdims=True)
    )


def mlp_forward(inputs, first_w, second_w, third_w, gain):
    pre_one = matmul(inputs, first_w)
    act_one = jax.nn.silu(pre_one).astype(jnp.bfloat16)
    pre_two = matmul(act_one, second_w)
    act_two = jax.nn.silu(pre_two).astype(jnp.bfloat16)
    normed, scale = norm_parts(matmul(act_two, third_w))
    return (normed * gain, (pre_one, act_one, pre_two, act_two, normed, scale))


def mlp_backward(inputs, first_w, second_w, third_w, gain, saved, upstream):
    pre_one, act_one, pre_two, act_two, normed, scale = saved
    grad_gain = jnp.sum(upstream * normed, axis=0)
    delta_out = norm_back(upstream * gain, normed, scale).astype(jnp.bfloat16)
    grad_third = over_rows(act_two, delta_out)
    delta_two = (against(delta_out, third_w) * silu_slope(pre_two)).astype(jnp.bfloat16)
    grad_second = over_rows(act_one, delta_two)
    delta_one = (against(delta_two, second_w) * silu_slope(pre_one)).astype(jnp.bfloat16)
    grad_first = over_rows(inputs, delta_one)
    return (against(delta_one, first_w), (grad_first, grad_second, grad_third, grad_gain))


def local_pass(
    node_lat, ghost_lat, edge_lat, node_cot, edge_cot, sender_ids, receiver_ids, counts, weights
):
    edge_one, edge_two, edge_three, edge_g, node_one, node_two, node_three, node_g = weights
    node_count = node_lat.shape[0]
    ghost_count = ghost_lat.shape[0]
    slot_count = ghost_count // 4
    latent = node_lat.shape[1]
    node_table = jnp.concatenate([node_lat, ghost_lat], axis=0)
    send_hot = (
        sender_ids[:, None] == lax.iota(jnp.int32, node_count + ghost_count)[None, :]
    ).astype(jnp.bfloat16)
    recv_hot = (receiver_ids[:, None] == lax.iota(jnp.int32, node_count)[None, :]).astype(
        jnp.bfloat16
    )
    sender_lat = matmul(send_hot, node_table).astype(jnp.bfloat16)
    receiver_lat = matmul(recv_hot, node_lat).astype(jnp.bfloat16)
    edge_in = jnp.concatenate([edge_lat, sender_lat, receiver_lat], axis=1)
    message, edge_saved = mlp_forward(edge_in, edge_one, edge_two, edge_three, edge_g)
    updated = (edge_lat.astype(jnp.float32) + message).astype(jnp.bfloat16)
    summed = over_rows(recv_hot, updated).astype(jnp.bfloat16)
    node_in = jnp.concatenate([node_lat, summed], axis=1)
    unused_out, node_saved = mlp_forward(node_in, node_one, node_two, node_three, node_g)
    node_up = node_cot.astype(jnp.float32)
    node_grad_in, node_terms = mlp_backward(
        node_in, node_one, node_two, node_three, node_g, node_saved, node_up
    )
    back_summed = node_grad_in[:, latent:].astype(jnp.bfloat16)
    edge_up = edge_cot.astype(jnp.float32) + matmul(recv_hot, back_summed)
    edge_grad_in, edge_terms = mlp_backward(
        edge_in, edge_one, edge_two, edge_three, edge_g, edge_saved, edge_up
    )
    grad_edge = (edge_up + edge_grad_in[:, :latent]).astype(jnp.bfloat16)
    to_sender = edge_grad_in[:, latent : 2 * latent].astype(jnp.bfloat16)
    to_receiver = edge_grad_in[:, 2 * latent :].astype(jnp.bfloat16)
    to_table = over_rows(send_hot, to_sender)
    node_total = (
        node_up
        + node_grad_in[:, :latent]
        + over_rows(recv_hot, to_receiver)
        + to_table[:node_count]
    )
    ghost_grad = to_table[node_count:].reshape(4, slot_count, latent)
    is_live = lax.iota(jnp.int32, slot_count)[None, :] < counts[:, None]
    ghost_grad = jnp.where(is_live[:, :, None], ghost_grad, 0.0).astype(jnp.bfloat16)
    return (grad_edge, node_total, ghost_grad, edge_terms + node_terms)


def per_device(
    node_latents,
    ghost_latents,
    edge_latents,
    node_cotangent,
    edge_cotangent,
    senders,
    receivers,
    halo_counts,
    recv_index,
    edge_w1,
    edge_w2,
    edge_w3,
    edge_gain,
    node_w1,
    node_w2,
    node_w3,
    node_gain,
):
    weights = (edge_w1, edge_w2, edge_w3, edge_gain, node_w1, node_w2, node_w3, node_gain)
    grad_edge, node_total, ghost_grad, grad_terms = local_pass(
        node_latents[0],
        ghost_latents[0],
        edge_latents[0],
        node_cotangent[0],
        edge_cotangent[0],
        senders[0],
        receivers[0],
        halo_counts[0],
        weights,
    )
    (
        edge_first,
        edge_second,
        edge_third,
        edge_gsum,
        node_first,
        node_second,
        node_third,
        node_gsum,
    ) = grad_terms
    domains = lax.axis_size("dom")
    groups = lax.axis_size("grp")
    reduced = (
        lax.psum_scatter(
            edge_first.astype(jnp.bfloat16), "grp", scatter_dimension=0, tiled=True
        ).astype(jnp.float32),
        lax.psum_scatter(
            edge_second.astype(jnp.bfloat16), "grp", scatter_dimension=0, tiled=True
        ).astype(jnp.float32),
        lax.psum_scatter(
            edge_third.astype(jnp.bfloat16), "grp", scatter_dimension=0, tiled=True
        ).astype(jnp.float32),
        lax.psum_scatter(
            edge_gsum.astype(jnp.bfloat16), "grp", scatter_dimension=0, tiled=True
        ).astype(jnp.float32),
        lax.psum_scatter(
            node_first.astype(jnp.bfloat16), "grp", scatter_dimension=0, tiled=True
        ).astype(jnp.float32),
        lax.psum_scatter(
            node_second.astype(jnp.bfloat16), "grp", scatter_dimension=0, tiled=True
        ).astype(jnp.float32),
        lax.psum_scatter(
            node_third.astype(jnp.bfloat16), "grp", scatter_dimension=0, tiled=True
        ).astype(jnp.float32),
        lax.psum_scatter(
            node_gsum.astype(jnp.bfloat16), "grp", scatter_dimension=0, tiled=True
        ).astype(jnp.float32),
    )
    reduced = lax.psum(
        (
            reduced[0],
            reduced[1],
            reduced[2],
            reduced[3],
            reduced[4],
            reduced[5],
            reduced[6],
            reduced[7],
        ),
        "dom",
    )
    arrivals = []
    for direction, offset in enumerate(OFFSETS):
        arrivals.append(from_behind(ghost_grad[direction], "dom", offset))
    arrived = jnp.stack(arrivals)
    node_count = node_total.shape[0]
    targets = recv_index[0].reshape(-1)
    owner_hot = (lax.iota(jnp.int32, node_count)[:, None] == targets[None, :]).astype(jnp.bfloat16)
    node_total = node_total + matmul(owner_hot, arrived.reshape(targets.shape[0], -1))
    grad_node = node_total.astype(jnp.bfloat16)[None]
    partitions = domains * groups
    edge_scale = 1.0 / math.sqrt(partitions * edge_latents.shape[1])
    node_scale = 1.0 / math.sqrt(partitions * node_latents.shape[1])
    return (
        grad_node,
        grad_edge[None],
        reduced[0] * edge_scale,
        reduced[1] * edge_scale,
        reduced[2] * edge_scale,
        reduced[3] * edge_scale,
        reduced[4] * node_scale,
        reduced[5] * node_scale,
        reduced[6] * node_scale,
        reduced[7] * node_scale,
    )


MESH = pl.DeviceIdType.MESH


def one_hot(mask):
    return jnp.where(mask, 1.0, 0.0).astype(jnp.bfloat16)


def hot_pair(ids, count):
    edges = ids.shape[1]
    column = jnp.transpose(jnp.broadcast_to(ids, (128, edges)))
    blocks = []
    for start in range(0, count, 128):
        width = min(128, count - start)
        lane = lax.broadcasted_iota(jnp.int32, (edges, width), 1) + start
        blocks.append(one_hot(column[:, :width] == lane))
    row = lax.broadcasted_iota(jnp.int32, (count, edges), 0)
    return blocks, one_hot(ids == row)


def wide(value):
    return value.astype(jnp.float32)


def narrow(value):
    return value.astype(jnp.bfloat16)


def activate(pre):
    sigma = jax.nn.sigmoid(pre)
    return narrow(pre * sigma), sigma * (1.0 + pre * (1.0 - sigma))


def fused_kernel(
    plan,
    node_lat_hbm,
    ghost_lat_hbm,
    edge_lat_hbm,
    node_cot_hbm,
    edge_cot_hbm,
    senders_hbm,
    receivers_hbm,
    counts_hbm,
    recv_index_hbm,
    ew1_hbm,
    ew2_hbm,
    ew3_hbm,
    egain_hbm,
    nw1_hbm,
    nw2_hbm,
    nw3_hbm,
    ngain_hbm,
    grad_node,
    grad_edge,
    out_e1,
    out_e2,
    out_e3,
    out_eg,
    out_n1,
    out_n2,
    out_n3,
    out_ng,
    terms_n,
    terms_b,
    terms_c,
    core_n,
    core_b,
    core_c,
    half_n,
    half_b,
    half_c,
    keep_n,
    keep_b,
    keep_c,
    side_n,
    side_b,
    side_c,
    part_n,
    part_b,
    part_c,
    gath_n,
    gath_b,
    gath_c,
    fin_n,
    fin_b,
    fin_c,
    ghost_out,
    ghost_in,
    send_sem,
    recv_sem,
    load_sem,
    node_lat,
    ghost_lat,
    edge_lat,
    node_cot,
    edge_cot,
    senders,
    receivers,
    counts,
    recv_index,
    ew1,
    ew2,
    ew3,
    egain,
    nw1,
    nw2,
    nw3,
    ngain,
):
    loads = {}
    for source, staged in (
        (senders_hbm, senders),
        (receivers_hbm, receivers),
        (node_lat_hbm, node_lat),
        (ghost_lat_hbm, ghost_lat),
        (edge_lat_hbm, edge_lat),
        (ew1_hbm, ew1),
        (ew2_hbm, ew2),
        (ew3_hbm, ew3),
        (egain_hbm, egain),
        (nw1_hbm, nw1),
        (nw2_hbm, nw2),
        (nw3_hbm, nw3),
        (node_cot_hbm, node_cot),
        (ngain_hbm, ngain),
        (edge_cot_hbm, edge_cot),
        (counts_hbm, counts),
        (recv_index_hbm, recv_index),
    ):
        load = pltpu.make_async_copy(source, staged, load_sem.at[len(loads)])
        load.start()
        loads[len(loads)] = load

    def need(first, last):
        for number in range(first, last):
            loads[number].wait()

    domains, edge_scale, node_scale = plan
    latent = node_lat.shape[1]
    owned = node_lat.shape[0]
    ghosts = ghost_lat.shape[0]
    slots = ghosts // 4
    blocks = domains // 2
    half = latent // 2
    dom = lax.axis_index("dom")
    grp = lax.axis_index("grp")
    core = lax.rem(grp, 2)
    pair = lax.div(grp, 2)
    other_core = 2 * pair + 1 - core
    other_pair = 2 * (1 - pair) + core
    per_chunk = 2 + 2 * (domains - 1)

    def ahead(step):
        return lax.rem(dom + step + domains, domains)

    barrier = pltpu.get_barrier_semaphore()
    pl.semaphore_signal(barrier, inc=1, device_id={"grp": other_core}, device_id_type=MESH)
    pl.semaphore_signal(barrier, inc=1, device_id={"grp": other_pair}, device_id_type=MESH)
    for step in range(1, domains):
        pl.semaphore_signal(barrier, inc=1, device_id={"dom": ahead(step)}, device_id_type=MESH)

    def remote(src, dst, number, target):
        return pltpu.make_async_remote_copy(
            src_ref=src,
            dst_ref=dst,
            send_sem=send_sem.at[number],
            recv_sem=recv_sem.at[number],
            device_id=target,
            device_id_type=MESH,
        )

    chunks = (
        (terms_n, core_n, half_n, keep_n, side_n, part_n, gath_n, fin_n),
        (terms_b, core_b, half_b, keep_b, side_b, part_b, gath_b, fin_b),
        (terms_c, core_c, half_c, keep_c, side_c, part_c, gath_c, fin_c),
    )

    def put(number, matrices, tail=None):
        terms = chunks[number][0]
        for quarter in range(4):
            rows = []
            for matrix in matrices:
                share = matrix.shape[0] // 4
                rows.append(matrix[quarter * share : (quarter + 1) * share])
            rows = narrow(rows[0] if len(rows) == 1 else jnp.concatenate(rows, axis=0))
            size = rows.shape[0] // blocks
            for piece in range(domains):
                at = (piece // 2) * size
                lane = (piece % 2) * half
                terms[quarter % 2, quarter // 2, piece, 0:size] = rows[
                    at : at + size, lane : lane + half
                ]
                if tail is not None:
                    terms[quarter % 2, quarter // 2, piece, size : size + 16] = tail

    def over_core(number):
        terms, arrived = chunks[number][0:2]
        return remote(
            terms.at[1 - core], arrived, number * per_chunk, {"grp": other_core}
        )

    def over_pair(number):
        return remote(
            chunks[number][2], chunks[number][4], number * per_chunk + 1, {"grp": other_pair}
        )

    def over_dom(number):
        part, gath = chunks[number][5:7]
        return [
            remote(
                part.at[ahead(step)],
                gath.at[step],
                number * per_chunk + 1 + step,
                {"dom": ahead(step)},
            )
            for step in range(1, domains)
        ]

    def spread(number):
        fin = chunks[number][7]
        return [
            remote(
                fin.at[0],
                fin.at[step],
                number * per_chunk + domains + step,
                {"dom": ahead(step)},
            )
            for step in range(1, domains)
        ]

    def stage_pair(number):
        terms, arrived, send, keep = chunks[number][0:4]
        over_core(number).wait()
        send[...] = narrow(wide(terms[core, 1 - pair]) + wide(arrived[1 - pair]))
        over_pair(number).start()
        keep[...] = wide(terms[core, pair]) + wide(arrived[pair])

    def stage_dom(number):
        keep, side, part = chunks[number][3:6]
        over_pair(number).wait()
        part[...] = narrow(keep[...] + wide(side[...]))
        for copy in over_dom(number):
            copy.start()

    def stage_spread(number):
        part, gath, fin = chunks[number][5:8]
        for copy in over_dom(number):
            copy.wait()
        total = wide(part[dom])
        for step in range(1, domains):
            total = total + wide(gath[step])
        fin[0] = narrow(total[: fin.shape[1]])
        for copy in spread(number):
            copy.start()
        return total

    def stage_out(number, outs, scale):
        fin = chunks[number][7]
        for copy in spread(number):
            copy.wait()
        size = fin.shape[1]
        for piece in range(domains):
            value = wide(fin[lax.rem(dom - piece + domains, domains)]) * scale
            lane = (piece % 2) * half
            first = (piece // 2) * size
            base = 0
            for out in outs:
                low, high = max(first, base), min(first + size, base + out.shape[0])
                if low < high:
                    out[low - base : high - base, lane : lane + half] = value[
                        low - first : high - first
                    ]
                base += out.shape[0]

    need(0, 2)
    sender_blocks, sender_rows = hot_pair(senders[...], owned + ghosts)
    receiver_blocks, receiver_rows = hot_pair(receivers[...], owned)
    receiver_hot = jnp.concatenate(receiver_blocks, axis=1)
    node_blocks = owned // 128
    sender_hot = jnp.concatenate(sender_blocks[:node_blocks], axis=1)
    ghost_hot = jnp.concatenate(sender_blocks[node_blocks:], axis=1)
    need(2, 5)
    own_lat = node_lat[...]
    edge_in0 = edge_lat[...]
    edge_in1 = narrow(matmul(sender_hot, own_lat) + matmul(ghost_hot, ghost_lat[...]))
    edge_in2 = narrow(matmul(receiver_hot, own_lat))

    need(5, 9)
    pre = (
        matmul(edge_in0, ew1[0:latent])
        + matmul(edge_in1, ew1[latent : 2 * latent])
        + matmul(edge_in2, ew1[2 * latent : 3 * latent])
    )
    e_act1, e_slope1 = activate(pre)
    e_act2, e_slope2 = activate(matmul(e_act1, ew2[...]))
    e_normed, e_norm = norm_parts(matmul(e_act2, ew3[...]))
    updated = narrow(wide(edge_in0) + e_normed * egain[...])
    summed = narrow(matmul(receiver_rows, updated))

    need(9, 17)
    pre = matmul(own_lat, nw1[0:latent]) + matmul(summed, nw1[latent : 2 * latent])
    n_act1, n_slope1 = activate(pre)
    n_act2, n_slope2 = activate(matmul(n_act1, nw2[...]))
    n_normed, n_norm = norm_parts(matmul(n_act2, nw3[...]))
    node_up = wide(node_cot[...])
    n_gsum = jnp.sum(node_up * n_normed, axis=0, keepdims=True)
    q3 = narrow(norm_back(node_up * ngain[...], n_normed, n_norm))
    q2 = narrow(against(q3, nw3[...]) * n_slope2)
    q1 = narrow(against(q2, nw2[...]) * n_slope1)
    back_summed = narrow(against(q1, nw1[latent : 2 * latent]))
    put(
        0,
        (
            jnp.concatenate([over_rows(own_lat, q1), over_rows(summed, q1)], axis=0),
            over_rows(n_act1, q2),
            over_rows(n_act2, q3),
        ),
    )
    pl.semaphore_wait(barrier, domains + 1)
    over_core(0).start()

    node_part = node_up + against(q1, nw1[0:latent])
    edge_up = wide(edge_cot[...]) + matmul(receiver_hot, back_summed)
    e_gsum = jnp.sum(edge_up * e_normed, axis=0, keepdims=True)
    q3 = narrow(norm_back(edge_up * egain[...], e_normed, e_norm))
    stage_pair(0)
    q2 = narrow(against(q3, ew3[...]) * e_slope2)
    row = lax.broadcasted_iota(jnp.int32, (16, half), 0)
    tail = jnp.where(row == 0, e_gsum[:, :half], 0.0)
    tail = jnp.where(row == 1, e_gsum[:, half:], tail)
    tail = jnp.where(row == 2, n_gsum[:, :half], tail)
    tail = narrow(jnp.where(row == 3, n_gsum[:, half:], tail))
    put(1, (over_rows(e_act1, q2), over_rows(e_act2, q3)), tail)
    over_core(1).start()
    q1 = narrow(against(q2, ew2[...]) * e_slope1)
    put(
        2,
        (
            jnp.concatenate(
                [over_rows(edge_in0, q1), over_rows(edge_in1, q1), over_rows(edge_in2, q1)],
                axis=0,
            ),
        ),
    )
    over_core(2).start()
    stage_pair(1)
    stage_dom(0)

    to_sender = narrow(against(q1, ew1[latent : 2 * latent]))
    to_table = matmul(sender_rows, to_sender)
    slot = lax.broadcasted_iota(jnp.int32, (slots, latent), 0)
    halos = []
    for direction, offset in enumerate(OFFSETS):
        first = owned + direction * slots
        live = slot < counts[:, direction : direction + 1]
        ghost_out[direction] = narrow(jnp.where(live, to_table[first : first + slots], 0.0))
        halo = remote(
            ghost_out.at[direction],
            ghost_in.at[direction],
            3 * per_chunk + direction,
            {"dom": ahead(offset)},
        )
        halo.start()
        halos.append(halo)
    stage_pair(2)
    stage_dom(1)
    to_receiver = narrow(against(q1, ew1[2 * latent : 3 * latent]))
    node_part = node_part + to_table[:owned] + matmul(receiver_rows, to_receiver)
    stage_spread(0)
    grad_edge[...] = narrow(edge_up + against(q1, ew1[0:latent]))
    stage_dom(2)
    gains = stage_spread(1)
    gains = gains[gains.shape[0] - 16 :]
    quarter = latent // 4
    for out, first, scale in ((out_eg, 0, edge_scale), (out_ng, 2, node_scale)):
        line = jnp.where(pair == 0, gains[first : first + 1], gains[first + 1 : first + 2])
        out[...] = jnp.where(core == 0, line[:, :quarter], line[:, quarter:]) * scale
    for halo in halos:
        halo.wait()
    owner = lax.broadcasted_iota(jnp.int32, (owned, slots), 0)
    for direction in range(4):
        hot = one_hot(owner == recv_index[direction : direction + 1, :])
        node_part = node_part + matmul(hot, ghost_in[direction])
    grad_node[...] = narrow(node_part)
    stage_out(0, (out_n1, out_n2, out_n3), node_scale)
    stage_spread(2)
    stage_out(1, (out_e2, out_e3), edge_scale)
    stage_out(2, (out_e1,), edge_scale)


def store_kernel(*refs):
    copies = [
        pltpu.make_async_copy(refs[at], refs[at + 10], refs[20].at[at]) for at in range(10)
    ]
    for copy in copies:
        copy.start()
    for copy in copies:
        copy.wait()


def fused_device(
    node_latents,
    ghost_latents,
    edge_latents,
    node_cotangent,
    edge_cotangent,
    senders,
    receivers,
    halo_counts,
    recv_index,
    edge_w1,
    edge_w2,
    edge_w3,
    edge_gain,
    node_w1,
    node_w2,
    node_w3,
    node_gain,
):
    domains = lax.axis_size("dom")
    groups = lax.axis_size("grp")
    nodes, latent = node_latents.shape[1:]
    edges = edge_latents.shape[1]
    slots = ghost_latents.shape[1] // 4
    partitions = domains * groups
    plan = (
        domains,
        1.0 / math.sqrt(partitions * edges),
        1.0 / math.sqrt(partitions * nodes),
    )
    half = latent // 2
    quarter = latent // 4
    blocks = domains // 2
    bulk = [
        node_w1.shape[0] // 4 + 2 * quarter,
        2 * quarter,
        edge_w1.shape[0] // 4,
    ]
    clean = [rows // blocks for rows in bulk]
    sizes = [clean[0], clean[1] + 16, clean[2]]

    def buffers(lead, kind, rows=sizes):
        return [pltpu.VMEM((*lead, size, half), kind) for size in rows]

    scratch = (
        buffers((2, 2, domains), jnp.bfloat16)
        + buffers((2, domains), jnp.bfloat16)
        + buffers((domains,), jnp.bfloat16)
        + buffers((domains,), jnp.float32)
        + buffers((domains,), jnp.bfloat16)
        + buffers((domains,), jnp.bfloat16)
        + buffers((domains,), jnp.bfloat16)
        + buffers((domains,), jnp.bfloat16, clean)
        + [
            pltpu.VMEM((4, slots, latent), jnp.bfloat16),
            pltpu.VMEM((4, slots, latent), jnp.bfloat16),
        ]
    )
    copies = 3 * (2 + 2 * (domains - 1)) + 4
    scratch += [pltpu.SemaphoreType.DMA((copies,)), pltpu.SemaphoreType.DMA((copies,))]
    operands = (
        node_latents[0],
        ghost_latents[0],
        edge_latents[0],
        node_cotangent[0],
        edge_cotangent[0],
        senders,
        receivers,
        halo_counts,
        recv_index[0],
        edge_w1,
        edge_w2,
        edge_w3,
        edge_gain[None],
        node_w1,
        node_w2,
        node_w3,
        node_gain[None],
    )
    scratch += [pltpu.SemaphoreType.DMA((len(operands),))]
    scratch += [pltpu.VMEM(operand.shape, operand.dtype) for operand in operands]
    vmem = pl.BlockSpec(memory_space=pltpu.VMEM)

    def grad(rows):
        return jax.ShapeDtypeStruct((rows, latent), jnp.float32)

    gain = jax.ShapeDtypeStruct((1, quarter), jnp.float32)
    outs = pl.pallas_call(
        functools.partial(fused_kernel, plan),
        out_shape=(
            jax.ShapeDtypeStruct((nodes, latent), jnp.bfloat16),
            jax.ShapeDtypeStruct((edges, latent), jnp.bfloat16),
            grad(edge_w1.shape[0] // 4),
            grad(quarter),
            grad(quarter),
            gain,
            grad(node_w1.shape[0] // 4),
            grad(quarter),
            grad(quarter),
            gain,
        ),
        in_specs=[pl.BlockSpec(memory_space=pltpu.HBM)] * len(operands),
        out_specs=[vmem] * 10,
        scratch_shapes=scratch,
        compiler_params=pltpu.CompilerParams(
            collective_id=0, has_side_effects=True, vmem_limit_bytes=60 * 1024 * 1024
        ),
    )(*operands)
    outs = pl.pallas_call(
        store_kernel,
        out_shape=tuple(jax.ShapeDtypeStruct(out.shape, out.dtype) for out in outs),
        in_specs=[pl.BlockSpec(memory_space=pltpu.HBM)] * 10,
        out_specs=[pl.BlockSpec(memory_space=pltpu.HBM)] * 10,
        scratch_shapes=[pltpu.SemaphoreType.DMA((10,))],
        compiler_params=pltpu.CompilerParams(vmem_limit_bytes=60 * 1024 * 1024),
    )(*outs)
    outs = list(outs)
    outs[0] = outs[0][None]
    outs[1] = outs[1][None]
    outs[5] = outs[5][0]
    outs[9] = outs[9][0]
    return tuple(outs)


def solution(mesh):
    placed = (
        P("grp", "dom", None),
        P("grp", "dom", None),
        P("grp", "dom", None),
        P("grp", "dom", None),
        P("grp", "dom", None),
        P("grp", "dom"),
        P("grp", "dom"),
        P("grp", "dom"),
        P("grp", "dom", None),
        P(),
        P(),
        P(),
        P(),
        P(),
        P(),
        P(),
        P(),
    )
    domains, groups = mesh.shape["dom"], mesh.shape["grp"]
    fits = groups == 4 and domains == 8
    return jax.shard_map(
        fused_device if fits else per_device,
        mesh=mesh,
        in_specs=placed,
        out_specs=(
            P("grp", "dom", None),
            P("grp", "dom", None),
            P("grp", None),
            P("grp", None),
            P("grp", None),
            P("grp"),
            P("grp", None),
            P("grp", None),
            P("grp", None),
            P("grp"),
        ),
        check_vma=False,
    )
```

```python
import functools
import math

import jax
import jax.numpy as jnp
from jax import lax
from jax.experimental import pallas as pl
from jax.experimental.pallas import tpu as pltpu
from jax.sharding import PartitionSpec as P

EPS = 1e-05
OFFSETS = (-2, -1, 1, 2)


def from_behind(block, axis, distance):
    devices = range(lax.axis_size(axis))
    route = [(i - distance, i) for i in devices if i - distance in devices]
    return lax.ppermute(block, axis, route)


def matmul(left, right):
    return jnp.dot(left, right, preferred_element_type=jnp.float32)


def over_rows(left, right):
    return lax.dot_general(
        left, right, (((0,), (0,)), ((), ())), preferred_element_type=jnp.float32
    )


def against(left, weight):
    return lax.dot_general(
        left, weight, (((1,), (1,)), ((), ())), preferred_element_type=jnp.float32
    )


def silu_slope(value):
    sigma = jax.nn.sigmoid(value)
    return sigma * (1.0 + value * (1.0 - sigma))


def norm_parts(value):
    centre = value - jnp.mean(value, axis=-1, keepdims=True)
    scale = lax.rsqrt(jnp.mean(centre * centre, axis=-1, keepdims=True) + EPS)
    return (centre * scale, scale)


def norm_back(upstream, normed, scale):
    return scale * (
        upstream
        - jnp.mean(upstream, axis=-1, keepdims=True)
        - normed * jnp.mean(upstream * normed, axis=-1, keepdims=True)
    )


def mlp_forward(inputs, first_w, second_w, third_w, gain):
    pre_one = matmul(inputs, first_w)
    act_one = jax.nn.silu(pre_one).astype(jnp.bfloat16)
    pre_two = matmul(act_one, second_w)
    act_two = jax.nn.silu(pre_two).astype(jnp.bfloat16)
    normed, scale = norm_parts(matmul(act_two, third_w))
    return (normed * gain, (pre_one, act_one, pre_two, act_two, normed, scale))


def mlp_backward(inputs, first_w, second_w, third_w, gain, saved, upstream):
    pre_one, act_one, pre_two, act_two, normed, scale = saved
    grad_gain = jnp.sum(upstream * normed, axis=0)
    delta_out = norm_back(upstream * gain, normed, scale).astype(jnp.bfloat16)
    grad_third = over_rows(act_two, delta_out)
    delta_two = (against(delta_out, third_w) * silu_slope(pre_two)).astype(jnp.bfloat16)
    grad_second = over_rows(act_one, delta_two)
    delta_one = (against(delta_two, second_w) * silu_slope(pre_one)).astype(jnp.bfloat16)
    grad_first = over_rows(inputs, delta_one)
    return (against(delta_one, first_w), (grad_first, grad_second, grad_third, grad_gain))


def local_pass(
    node_lat, ghost_lat, edge_lat, node_cot, edge_cot, sender_ids, receiver_ids, counts, weights
):
    edge_one, edge_two, edge_three, edge_g, node_one, node_two, node_three, node_g = weights
    node_count = node_lat.shape[0]
    ghost_count = ghost_lat.shape[0]
    slot_count = ghost_count // 4
    latent = node_lat.shape[1]
    node_table = jnp.concatenate([node_lat, ghost_lat], axis=0)
    send_hot = (
        sender_ids[:, None] == lax.iota(jnp.int32, node_count + ghost_count)[None, :]
    ).astype(jnp.bfloat16)
    recv_hot = (receiver_ids[:, None] == lax.iota(jnp.int32, node_count)[None, :]).astype(
        jnp.bfloat16
    )
    sender_lat = matmul(send_hot, node_table).astype(jnp.bfloat16)
    receiver_lat = matmul(recv_hot, node_lat).astype(jnp.bfloat16)
    edge_in = jnp.concatenate([edge_lat, sender_lat, receiver_lat], axis=1)
    message, edge_saved = mlp_forward(edge_in, edge_one, edge_two, edge_three, edge_g)
    updated = (edge_lat.astype(jnp.float32) + message).astype(jnp.bfloat16)
    summed = over_rows(recv_hot, updated).astype(jnp.bfloat16)
    node_in = jnp.concatenate([node_lat, summed], axis=1)
    unused_out, node_saved = mlp_forward(node_in, node_one, node_two, node_three, node_g)
    node_up = node_cot.astype(jnp.float32)
    node_grad_in, node_terms = mlp_backward(
        node_in, node_one, node_two, node_three, node_g, node_saved, node_up
    )
    back_summed = node_grad_in[:, latent:].astype(jnp.bfloat16)
    edge_up = edge_cot.astype(jnp.float32) + matmul(recv_hot, back_summed)
    edge_grad_in, edge_terms = mlp_backward(
        edge_in, edge_one, edge_two, edge_three, edge_g, edge_saved, edge_up
    )
    grad_edge = (edge_up + edge_grad_in[:, :latent]).astype(jnp.bfloat16)
    to_sender = edge_grad_in[:, latent : 2 * latent].astype(jnp.bfloat16)
    to_receiver = edge_grad_in[:, 2 * latent :].astype(jnp.bfloat16)
    to_table = over_rows(send_hot, to_sender)
    node_total = (
        node_up
        + node_grad_in[:, :latent]
        + over_rows(recv_hot, to_receiver)
        + to_table[:node_count]
    )
    ghost_grad = to_table[node_count:].reshape(4, slot_count, latent)
    is_live = lax.iota(jnp.int32, slot_count)[None, :] < counts[:, None]
    ghost_grad = jnp.where(is_live[:, :, None], ghost_grad, 0.0).astype(jnp.bfloat16)
    return (grad_edge, node_total, ghost_grad, edge_terms + node_terms)


def per_device(
    node_latents,
    ghost_latents,
    edge_latents,
    node_cotangent,
    edge_cotangent,
    senders,
    receivers,
    halo_counts,
    recv_index,
    edge_w1,
    edge_w2,
    edge_w3,
    edge_gain,
    node_w1,
    node_w2,
    node_w3,
    node_gain,
):
    weights = (edge_w1, edge_w2, edge_w3, edge_gain, node_w1, node_w2, node_w3, node_gain)
    grad_edge, node_total, ghost_grad, grad_terms = local_pass(
        node_latents[0],
        ghost_latents[0],
        edge_latents[0],
        node_cotangent[0],
        edge_cotangent[0],
        senders[0],
        receivers[0],
        halo_counts[0],
        weights,
    )
    (
        edge_first,
        edge_second,
        edge_third,
        edge_gsum,
        node_first,
        node_second,
        node_third,
        node_gsum,
    ) = grad_terms
    domains = lax.axis_size("dom")
    groups = lax.axis_size("grp")
    reduced = (
        lax.psum_scatter(
            edge_first.astype(jnp.bfloat16), "grp", scatter_dimension=0, tiled=True
        ).astype(jnp.float32),
        lax.psum_scatter(
            edge_second.astype(jnp.bfloat16), "grp", scatter_dimension=0, tiled=True
        ).astype(jnp.float32),
        lax.psum_scatter(
            edge_third.astype(jnp.bfloat16), "grp", scatter_dimension=0, tiled=True
        ).astype(jnp.float32),
        lax.psum_scatter(
            edge_gsum.astype(jnp.bfloat16), "grp", scatter_dimension=0, tiled=True
        ).astype(jnp.float32),
        lax.psum_scatter(
            node_first.astype(jnp.bfloat16), "grp", scatter_dimension=0, tiled=True
        ).astype(jnp.float32),
        lax.psum_scatter(
            node_second.astype(jnp.bfloat16), "grp", scatter_dimension=0, tiled=True
        ).astype(jnp.float32),
        lax.psum_scatter(
            node_third.astype(jnp.bfloat16), "grp", scatter_dimension=0, tiled=True
        ).astype(jnp.float32),
        lax.psum_scatter(
            node_gsum.astype(jnp.bfloat16), "grp", scatter_dimension=0, tiled=True
        ).astype(jnp.float32),
    )
    reduced = lax.psum(
        (
            reduced[0],
            reduced[1],
            reduced[2],
            reduced[3],
            reduced[4],
            reduced[5],
            reduced[6],
            reduced[7],
        ),
        "dom",
    )
    arrivals = []
    for direction, offset in enumerate(OFFSETS):
        arrivals.append(from_behind(ghost_grad[direction], "dom", offset))
    arrived = jnp.stack(arrivals)
    node_count = node_total.shape[0]
    targets = recv_index[0].reshape(-1)
    owner_hot = (lax.iota(jnp.int32, node_count)[:, None] == targets[None, :]).astype(jnp.bfloat16)
    node_total = node_total + matmul(owner_hot, arrived.reshape(targets.shape[0], -1))
    grad_node = node_total.astype(jnp.bfloat16)[None]
    partitions = domains * groups
    edge_scale = 1.0 / math.sqrt(partitions * edge_latents.shape[1])
    node_scale = 1.0 / math.sqrt(partitions * node_latents.shape[1])
    return (
        grad_node,
        grad_edge[None],
        reduced[0] * edge_scale,
        reduced[1] * edge_scale,
        reduced[2] * edge_scale,
        reduced[3] * edge_scale,
        reduced[4] * node_scale,
        reduced[5] * node_scale,
        reduced[6] * node_scale,
        reduced[7] * node_scale,
    )


MESH = pl.DeviceIdType.MESH


def one_hot(mask):
    return jnp.where(mask, 1.0, 0.0).astype(jnp.bfloat16)


def hot_pair(ids, count):
    edges = ids.shape[1]
    column = jnp.transpose(jnp.broadcast_to(ids, (128, edges)))
    blocks = []
    for start in range(0, count, 128):
        width = min(128, count - start)
        lane = lax.broadcasted_iota(jnp.int32, (edges, width), 1) + start
        blocks.append(one_hot(column[:, :width] == lane))
    row = lax.broadcasted_iota(jnp.int32, (count, edges), 0)
    return blocks, one_hot(ids == row)


def wide(value):
    return value.astype(jnp.float32)


def narrow(value):
    return value.astype(jnp.bfloat16)


def activate(pre):
    sigma = jax.nn.sigmoid(pre)
    return narrow(pre * sigma), sigma * (1.0 + pre * (1.0 - sigma))


def fused_kernel(
    plan,
    node_lat_hbm,
    ghost_lat_hbm,
    edge_lat_hbm,
    node_cot_hbm,
    edge_cot_hbm,
    senders_hbm,
    receivers_hbm,
    counts_hbm,
    recv_index_hbm,
    ew1_hbm,
    ew2_hbm,
    ew3_hbm,
    egain_hbm,
    nw1_hbm,
    nw2_hbm,
    nw3_hbm,
    ngain_hbm,
    grad_node,
    grad_edge,
    out_e1,
    out_e2,
    out_e3,
    out_eg,
    out_n1,
    out_n2,
    out_n3,
    out_ng,
    terms_n,
    terms_b,
    terms_c,
    core_n,
    core_b,
    core_c,
    half_n,
    half_b,
    half_c,
    keep_n,
    keep_b,
    keep_c,
    side_n,
    side_b,
    side_c,
    part_n,
    part_b,
    part_c,
    gath_n,
    gath_b,
    gath_c,
    fin_n,
    fin_b,
    fin_c,
    ghost_out,
    ghost_in,
    send_sem,
    recv_sem,
    load_sem,
    node_lat,
    ghost_lat,
    edge_lat,
    node_cot,
    edge_cot,
    senders,
    receivers,
    counts,
    recv_index,
    ew1,
    ew2,
    ew3,
    egain,
    nw1,
    nw2,
    nw3,
    ngain,
):
    loads = {}
    for source, staged in (
        (senders_hbm, senders),
        (receivers_hbm, receivers),
        (node_lat_hbm, node_lat),
        (ghost_lat_hbm, ghost_lat),
        (edge_lat_hbm, edge_lat),
        (ew1_hbm, ew1),
        (ew2_hbm, ew2),
        (ew3_hbm, ew3),
        (egain_hbm, egain),
        (nw1_hbm, nw1),
        (nw2_hbm, nw2),
        (nw3_hbm, nw3),
        (node_cot_hbm, node_cot),
        (ngain_hbm, ngain),
        (edge_cot_hbm, edge_cot),
        (counts_hbm, counts),
        (recv_index_hbm, recv_index),
    ):
        load = pltpu.make_async_copy(source, staged, load_sem.at[len(loads)])
        load.start()
        loads[len(loads)] = load

    def need(first, last):
        for number in range(first, last):
            loads[number].wait()

    domains, edge_scale, node_scale = plan
    latent = node_lat.shape[1]
    owned = node_lat.shape[0]
    ghosts = ghost_lat.shape[0]
    slots = ghosts // 4
    blocks = domains // 2
    half = latent // 2
    dom = lax.axis_index("dom")
    grp = lax.axis_index("grp")
    core = lax.rem(grp, 2)
    pair = lax.div(grp, 2)
    other_core = 2 * pair + 1 - core
    other_pair = 2 * (1 - pair) + core
    per_chunk = 2 + 2 * (domains - 1)

    def ahead(step):
        return lax.rem(dom + step + domains, domains)

    barrier = pltpu.get_barrier_semaphore()
    pl.semaphore_signal(barrier, inc=1, device_id={"grp": other_core}, device_id_type=MESH)
    pl.semaphore_signal(barrier, inc=1, device_id={"grp": other_pair}, device_id_type=MESH)
    for step in range(1, domains):
        pl.semaphore_signal(barrier, inc=1, device_id={"dom": ahead(step)}, device_id_type=MESH)

    def remote(src, dst, number, target):
        return pltpu.make_async_remote_copy(
            src_ref=src,
            dst_ref=dst,
            send_sem=send_sem.at[number],
            recv_sem=recv_sem.at[number],
            device_id=target,
            device_id_type=MESH,
        )

    chunks = (
        (terms_n, core_n, half_n, keep_n, side_n, part_n, gath_n, fin_n),
        (terms_b, core_b, half_b, keep_b, side_b, part_b, gath_b, fin_b),
        (terms_c, core_c, half_c, keep_c, side_c, part_c, gath_c, fin_c),
    )

    def put(number, matrices, tail=None):
        terms = chunks[number][0]
        for quarter in range(4):
            rows = []
            for matrix in matrices:
                share = matrix.shape[0] // 4
                rows.append(matrix[quarter * share : (quarter + 1) * share])
            rows = narrow(rows[0] if len(rows) == 1 else jnp.concatenate(rows, axis=0))
            size = rows.shape[0] // blocks
            for piece in range(domains):
                at = (piece // 2) * size
                lane = (piece % 2) * half
                terms[quarter % 2, quarter // 2, piece, 0:size] = rows[
                    at : at + size, lane : lane + half
                ]
                if tail is not None:
                    terms[quarter % 2, quarter // 2, piece, size : size + 16] = tail

    def over_core(number):
        terms, arrived = chunks[number][0:2]
        return remote(
            terms.at[1 - core], arrived, number * per_chunk, {"grp": other_core}
        )

    def over_pair(number):
        return remote(
            chunks[number][2], chunks[number][4], number * per_chunk + 1, {"grp": other_pair}
        )

    def over_dom(number):
        part, gath = chunks[number][5:7]
        return [
            remote(
                part.at[ahead(step)],
                gath.at[step],
                number * per_chunk + 1 + step,
                {"dom": ahead(step)},
            )
            for step in range(1, domains)
        ]

    def spread(number):
        fin = chunks[number][7]
        return [
            remote(
                fin.at[0],
                fin.at[step],
                number * per_chunk + domains + step,
                {"dom": ahead(step)},
            )
            for step in range(1, domains)
        ]

    def stage_pair(number):
        terms, arrived, send, keep = chunks[number][0:4]
        over_core(number).wait()
        send[...] = narrow(wide(terms[core, 1 - pair]) + wide(arrived[1 - pair]))
        over_pair(number).start()
        keep[...] = wide(terms[core, pair]) + wide(arrived[pair])

    def stage_dom(number):
        keep, side, part = chunks[number][3:6]
        over_pair(number).wait()
        part[...] = narrow(keep[...] + wide(side[...]))
        for copy in over_dom(number):
            copy.start()

    def stage_spread(number):
        part, gath, fin = chunks[number][5:8]
        for copy in over_dom(number):
            copy.wait()
        total = wide(part[dom])
        for step in range(1, domains):
            total = total + wide(gath[step])
        fin[0] = narrow(total[: fin.shape[1]])
        for copy in spread(number):
            copy.start()
        return total

    def stage_out(number, outs, scale):
        fin = chunks[number][7]
        for copy in spread(number):
            copy.wait()
        size = fin.shape[1]
        for piece in range(domains):
            value = wide(fin[lax.rem(dom - piece + domains, domains)]) * scale
            lane = (piece % 2) * half
            first = (piece // 2) * size
            base = 0
            for out in outs:
                low, high = max(first, base), min(first + size, base + out.shape[0])
                if low < high:
                    out[low - base : high - base, lane : lane + half] = value[
                        low - first : high - first
                    ]
                base += out.shape[0]

    need(0, 2)
    sender_blocks, sender_rows = hot_pair(senders[...], owned + ghosts)
    receiver_blocks, receiver_rows = hot_pair(receivers[...], owned)
    receiver_hot = jnp.concatenate(receiver_blocks, axis=1)
    node_blocks = owned // 128
    sender_hot = jnp.concatenate(sender_blocks[:node_blocks], axis=1)
    ghost_hot = jnp.concatenate(sender_blocks[node_blocks:], axis=1)
    need(2, 5)
    own_lat = node_lat[...]
    edge_in0 = edge_lat[...]
    edge_in1 = narrow(matmul(sender_hot, own_lat) + matmul(ghost_hot, ghost_lat[...]))
    edge_in2 = narrow(matmul(receiver_hot, own_lat))

    need(5, 9)
    pre = (
        matmul(edge_in0, ew1[0:latent])
        + matmul(edge_in1, ew1[latent : 2 * latent])
        + matmul(edge_in2, ew1[2 * latent : 3 * latent])
    )
    e_act1, e_slope1 = activate(pre)
    e_act2, e_slope2 = activate(matmul(e_act1, ew2[...]))
    e_normed, e_norm = norm_parts(matmul(e_act2, ew3[...]))
    updated = narrow(wide(edge_in0) + e_normed * egain[...])
    summed = narrow(matmul(receiver_rows, updated))

    need(9, 17)
    pre = matmul(own_lat, nw1[0:latent]) + matmul(summed, nw1[latent : 2 * latent])
    n_act1, n_slope1 = activate(pre)
    n_act2, n_slope2 = activate(matmul(n_act1, nw2[...]))
    n_normed, n_norm = norm_parts(matmul(n_act2, nw3[...]))
    node_up = wide(node_cot[...])
    n_gsum = jnp.sum(node_up * n_normed, axis=0, keepdims=True)
    q3 = narrow(norm_back(node_up * ngain[...], n_normed, n_norm))
    q2 = narrow(against(q3, nw3[...]) * n_slope2)
    q1 = narrow(against(q2, nw2[...]) * n_slope1)
    back_summed = narrow(against(q1, nw1[latent : 2 * latent]))
    put(
        0,
        (
            jnp.concatenate([over_rows(own_lat, q1), over_rows(summed, q1)], axis=0),
            over_rows(n_act1, q2),
            over_rows(n_act2, q3),
        ),
    )
    pl.semaphore_wait(barrier, domains + 1)
    over_core(0).start()

    node_part = node_up + against(q1, nw1[0:latent])
    edge_up = wide(edge_cot[...]) + matmul(receiver_hot, back_summed)
    e_gsum = jnp.sum(edge_up * e_normed, axis=0, keepdims=True)
    q3 = narrow(norm_back(edge_up * egain[...], e_normed, e_norm))
    stage_pair(0)
    q2 = narrow(against(q3, ew3[...]) * e_slope2)
    row = lax.broadcasted_iota(jnp.int32, (16, half), 0)
    tail = jnp.where(row == 0, e_gsum[:, :half], 0.0)
    tail = jnp.where(row == 1, e_gsum[:, half:], tail)
    tail = jnp.where(row == 2, n_gsum[:, :half], tail)
    tail = narrow(jnp.where(row == 3, n_gsum[:, half:], tail))
    put(1, (over_rows(e_act1, q2), over_rows(e_act2, q3)), tail)
    over_core(1).start()
    q1 = narrow(against(q2, ew2[...]) * e_slope1)
    stage_dom(0)
    put(
        2,
        (
            jnp.concatenate(
                [over_rows(edge_in0, q1), over_rows(edge_in1, q1), over_rows(edge_in2, q1)],
                axis=0,
            ),
        ),
    )
    over_core(2).start()
    stage_pair(1)

    to_sender = narrow(against(q1, ew1[latent : 2 * latent]))
    to_table = matmul(sender_rows, to_sender)
    slot = lax.broadcasted_iota(jnp.int32, (slots, latent), 0)
    halos = []
    for direction, offset in enumerate(OFFSETS):
        first = owned + direction * slots
        live = slot < counts[:, direction : direction + 1]
        ghost_out[direction] = narrow(jnp.where(live, to_table[first : first + slots], 0.0))
        halo = remote(
            ghost_out.at[direction],
            ghost_in.at[direction],
            3 * per_chunk + direction,
            {"dom": ahead(offset)},
        )
        halo.start()
        halos.append(halo)
    stage_pair(2)
    stage_dom(1)
    to_receiver = narrow(against(q1, ew1[2 * latent : 3 * latent]))
    node_part = node_part + to_table[:owned] + matmul(receiver_rows, to_receiver)
    stage_spread(0)
    grad_edge[...] = narrow(edge_up + against(q1, ew1[0:latent]))
    stage_dom(2)
    gains = stage_spread(1)
    gains = gains[gains.shape[0] - 16 :]
    quarter = latent // 4
    for out, first, scale in ((out_eg, 0, edge_scale), (out_ng, 2, node_scale)):
        line = jnp.where(pair == 0, gains[first : first + 1], gains[first + 1 : first + 2])
        out[...] = jnp.where(core == 0, line[:, :quarter], line[:, quarter:]) * scale
    for halo in halos:
        halo.wait()
    owner = lax.broadcasted_iota(jnp.int32, (owned, slots), 0)
    for direction in range(4):
        hot = one_hot(owner == recv_index[direction : direction + 1, :])
        node_part = node_part + matmul(hot, ghost_in[direction])
    grad_node[...] = narrow(node_part)
    stage_out(0, (out_n1, out_n2, out_n3), node_scale)
    stage_spread(2)
    stage_out(1, (out_e2, out_e3), edge_scale)
    stage_out(2, (out_e1,), edge_scale)


def store_kernel(*refs):
    ins, outs, held = refs[:10], refs[10:20], refs[20:30]
    load_sem, store_sem = refs[30:]
    loads = [pltpu.make_async_copy(ins[at], held[at], load_sem.at[at]) for at in range(10)]
    stores = [pltpu.make_async_copy(held[at], outs[at], store_sem.at[at]) for at in range(10)]
    for load in loads:
        load.start()
    for load, store in zip(loads, stores):
        load.wait()
        store.start()
    for store in stores:
        store.wait()


def fused_device(
    node_latents,
    ghost_latents,
    edge_latents,
    node_cotangent,
    edge_cotangent,
    senders,
    receivers,
    halo_counts,
    recv_index,
    edge_w1,
    edge_w2,
    edge_w3,
    edge_gain,
    node_w1,
    node_w2,
    node_w3,
    node_gain,
):
    domains = lax.axis_size("dom")
    groups = lax.axis_size("grp")
    nodes, latent = node_latents.shape[1:]
    edges = edge_latents.shape[1]
    slots = ghost_latents.shape[1] // 4
    partitions = domains * groups
    plan = (
        domains,
        1.0 / math.sqrt(partitions * edges),
        1.0 / math.sqrt(partitions * nodes),
    )
    half = latent // 2
    quarter = latent // 4
    blocks = domains // 2
    bulk = [
        node_w1.shape[0] // 4 + 2 * quarter,
        2 * quarter,
        edge_w1.shape[0] // 4,
    ]
    clean = [rows // blocks for rows in bulk]
    sizes = [clean[0], clean[1] + 16, clean[2]]

    def buffers(lead, kind, rows=sizes):
        return [pltpu.VMEM((*lead, size, half), kind) for size in rows]

    scratch = (
        buffers((2, 2, domains), jnp.bfloat16)
        + buffers((2, domains), jnp.bfloat16)
        + buffers((domains,), jnp.bfloat16)
        + buffers((domains,), jnp.float32)
        + buffers((domains,), jnp.bfloat16)
        + buffers((domains,), jnp.bfloat16)
        + buffers((domains,), jnp.bfloat16)
        + buffers((domains,), jnp.bfloat16, clean)
        + [
            pltpu.VMEM((4, slots, latent), jnp.bfloat16),
            pltpu.VMEM((4, slots, latent), jnp.bfloat16),
        ]
    )
    copies = 3 * (2 + 2 * (domains - 1)) + 4
    scratch += [pltpu.SemaphoreType.DMA((copies,)), pltpu.SemaphoreType.DMA((copies,))]
    operands = (
        node_latents[0],
        ghost_latents[0],
        edge_latents[0],
        node_cotangent[0],
        edge_cotangent[0],
        senders,
        receivers,
        halo_counts,
        recv_index[0],
        edge_w1,
        edge_w2,
        edge_w3,
        edge_gain[None],
        node_w1,
        node_w2,
        node_w3,
        node_gain[None],
    )
    scratch += [pltpu.SemaphoreType.DMA((len(operands),))]
    scratch += [pltpu.VMEM(operand.shape, operand.dtype) for operand in operands]
    vmem = pl.BlockSpec(memory_space=pltpu.VMEM)

    def grad(rows):
        return jax.ShapeDtypeStruct((rows, latent), jnp.float32)

    gain = jax.ShapeDtypeStruct((1, quarter), jnp.float32)
    outs = pl.pallas_call(
        functools.partial(fused_kernel, plan),
        out_shape=(
            jax.ShapeDtypeStruct((nodes, latent), jnp.bfloat16),
            jax.ShapeDtypeStruct((edges, latent), jnp.bfloat16),
            grad(edge_w1.shape[0] // 4),
            grad(quarter),
            grad(quarter),
            gain,
            grad(node_w1.shape[0] // 4),
            grad(quarter),
            grad(quarter),
            gain,
        ),
        in_specs=[pl.BlockSpec(memory_space=pltpu.HBM)] * len(operands),
        out_specs=[vmem] * 10,
        scratch_shapes=scratch,
        compiler_params=pltpu.CompilerParams(
            collective_id=0, has_side_effects=True, vmem_limit_bytes=60 * 1024 * 1024
        ),
    )(*operands)
    outs = pl.pallas_call(
        store_kernel,
        out_shape=tuple(jax.ShapeDtypeStruct(out.shape, out.dtype) for out in outs),
        in_specs=[pl.BlockSpec(memory_space=pltpu.HBM)] * 10,
        out_specs=[pl.BlockSpec(memory_space=pltpu.HBM)] * 10,
        scratch_shapes=[pltpu.VMEM(out.shape, out.dtype) for out in outs]
        + [pltpu.SemaphoreType.DMA((10,)), pltpu.SemaphoreType.DMA((10,))],
        compiler_params=pltpu.CompilerParams(vmem_limit_bytes=60 * 1024 * 1024),
    )(*outs)
    outs = list(outs)
    outs[0] = outs[0][None]
    outs[1] = outs[1][None]
    outs[5] = outs[5][0]
    outs[9] = outs[9][0]
    return tuple(outs)


def solution(mesh):
    placed = (
        P("grp", "dom", None),
        P("grp", "dom", None),
        P("grp", "dom", None),
        P("grp", "dom", None),
        P("grp", "dom", None),
        P("grp", "dom"),
        P("grp", "dom"),
        P("grp", "dom"),
        P("grp", "dom", None),
        P(),
        P(),
        P(),
        P(),
        P(),
        P(),
        P(),
        P(),
    )
    domains, groups = mesh.shape["dom"], mesh.shape["grp"]
    fits = groups == 4 and domains == 8
    return jax.shard_map(
        fused_device if fits else per_device,
        mesh=mesh,
        in_specs=placed,
        out_specs=(
            P("grp", "dom", None),
            P("grp", "dom", None),
            P("grp", None),
            P("grp", None),
            P("grp", None),
            P("grp"),
            P("grp", None),
            P("grp", None),
            P("grp", None),
            P("grp"),
        ),
        check_vma=False,
    )
```

```python
import functools
import math

import jax
import jax.numpy as jnp
from jax import lax
from jax.experimental import pallas as pl
from jax.experimental.pallas import tpu as pltpu
from jax.sharding import PartitionSpec as P

EPS = 1e-05
OFFSETS = (-2, -1, 1, 2)


def from_behind(block, axis, distance):
    devices = range(lax.axis_size(axis))
    route = [(i - distance, i) for i in devices if i - distance in devices]
    return lax.ppermute(block, axis, route)


def matmul(left, right):
    return jnp.dot(left, right, preferred_element_type=jnp.float32)


def over_rows(left, right):
    return lax.dot_general(
        left, right, (((0,), (0,)), ((), ())), preferred_element_type=jnp.float32
    )


def against(left, weight):
    return lax.dot_general(
        left, weight, (((1,), (1,)), ((), ())), preferred_element_type=jnp.float32
    )


def silu_slope(value):
    sigma = jax.nn.sigmoid(value)
    return sigma * (1.0 + value * (1.0 - sigma))


def norm_parts(value):
    centre = value - jnp.mean(value, axis=-1, keepdims=True)
    scale = lax.rsqrt(jnp.mean(centre * centre, axis=-1, keepdims=True) + EPS)
    return (centre * scale, scale)


def norm_back(upstream, normed, scale):
    return scale * (
        upstream
        - jnp.mean(upstream, axis=-1, keepdims=True)
        - normed * jnp.mean(upstream * normed, axis=-1, keepdims=True)
    )


def mlp_forward(inputs, first_w, second_w, third_w, gain):
    pre_one = matmul(inputs, first_w)
    act_one = jax.nn.silu(pre_one).astype(jnp.bfloat16)
    pre_two = matmul(act_one, second_w)
    act_two = jax.nn.silu(pre_two).astype(jnp.bfloat16)
    normed, scale = norm_parts(matmul(act_two, third_w))
    return (normed * gain, (pre_one, act_one, pre_two, act_two, normed, scale))


def mlp_backward(inputs, first_w, second_w, third_w, gain, saved, upstream):
    pre_one, act_one, pre_two, act_two, normed, scale = saved
    grad_gain = jnp.sum(upstream * normed, axis=0)
    delta_out = norm_back(upstream * gain, normed, scale).astype(jnp.bfloat16)
    grad_third = over_rows(act_two, delta_out)
    delta_two = (against(delta_out, third_w) * silu_slope(pre_two)).astype(jnp.bfloat16)
    grad_second = over_rows(act_one, delta_two)
    delta_one = (against(delta_two, second_w) * silu_slope(pre_one)).astype(jnp.bfloat16)
    grad_first = over_rows(inputs, delta_one)
    return (against(delta_one, first_w), (grad_first, grad_second, grad_third, grad_gain))


def local_pass(
    node_lat, ghost_lat, edge_lat, node_cot, edge_cot, sender_ids, receiver_ids, counts, weights
):
    edge_one, edge_two, edge_three, edge_g, node_one, node_two, node_three, node_g = weights
    node_count = node_lat.shape[0]
    ghost_count = ghost_lat.shape[0]
    slot_count = ghost_count // 4
    latent = node_lat.shape[1]
    node_table = jnp.concatenate([node_lat, ghost_lat], axis=0)
    send_hot = (
        sender_ids[:, None] == lax.iota(jnp.int32, node_count + ghost_count)[None, :]
    ).astype(jnp.bfloat16)
    recv_hot = (receiver_ids[:, None] == lax.iota(jnp.int32, node_count)[None, :]).astype(
        jnp.bfloat16
    )
    sender_lat = matmul(send_hot, node_table).astype(jnp.bfloat16)
    receiver_lat = matmul(recv_hot, node_lat).astype(jnp.bfloat16)
    edge_in = jnp.concatenate([edge_lat, sender_lat, receiver_lat], axis=1)
    message, edge_saved = mlp_forward(edge_in, edge_one, edge_two, edge_three, edge_g)
    updated = (edge_lat.astype(jnp.float32) + message).astype(jnp.bfloat16)
    summed = over_rows(recv_hot, updated).astype(jnp.bfloat16)
    node_in = jnp.concatenate([node_lat, summed], axis=1)
    unused_out, node_saved = mlp_forward(node_in, node_one, node_two, node_three, node_g)
    node_up = node_cot.astype(jnp.float32)
    node_grad_in, node_terms = mlp_backward(
        node_in, node_one, node_two, node_three, node_g, node_saved, node_up
    )
    back_summed = node_grad_in[:, latent:].astype(jnp.bfloat16)
    edge_up = edge_cot.astype(jnp.float32) + matmul(recv_hot, back_summed)
    edge_grad_in, edge_terms = mlp_backward(
        edge_in, edge_one, edge_two, edge_three, edge_g, edge_saved, edge_up
    )
    grad_edge = (edge_up + edge_grad_in[:, :latent]).astype(jnp.bfloat16)
    to_sender = edge_grad_in[:, latent : 2 * latent].astype(jnp.bfloat16)
    to_receiver = edge_grad_in[:, 2 * latent :].astype(jnp.bfloat16)
    to_table = over_rows(send_hot, to_sender)
    node_total = (
        node_up
        + node_grad_in[:, :latent]
        + over_rows(recv_hot, to_receiver)
        + to_table[:node_count]
    )
    ghost_grad = to_table[node_count:].reshape(4, slot_count, latent)
    is_live = lax.iota(jnp.int32, slot_count)[None, :] < counts[:, None]
    ghost_grad = jnp.where(is_live[:, :, None], ghost_grad, 0.0).astype(jnp.bfloat16)
    return (grad_edge, node_total, ghost_grad, edge_terms + node_terms)


def per_device(
    node_latents,
    ghost_latents,
    edge_latents,
    node_cotangent,
    edge_cotangent,
    senders,
    receivers,
    halo_counts,
    recv_index,
    edge_w1,
    edge_w2,
    edge_w3,
    edge_gain,
    node_w1,
    node_w2,
    node_w3,
    node_gain,
):
    weights = (edge_w1, edge_w2, edge_w3, edge_gain, node_w1, node_w2, node_w3, node_gain)
    grad_edge, node_total, ghost_grad, grad_terms = local_pass(
        node_latents[0],
        ghost_latents[0],
        edge_latents[0],
        node_cotangent[0],
        edge_cotangent[0],
        senders[0],
        receivers[0],
        halo_counts[0],
        weights,
    )
    (
        edge_first,
        edge_second,
        edge_third,
        edge_gsum,
        node_first,
        node_second,
        node_third,
        node_gsum,
    ) = grad_terms
    domains = lax.axis_size("dom")
    groups = lax.axis_size("grp")
    reduced = (
        lax.psum_scatter(
            edge_first.astype(jnp.bfloat16), "grp", scatter_dimension=0, tiled=True
        ).astype(jnp.float32),
        lax.psum_scatter(
            edge_second.astype(jnp.bfloat16), "grp", scatter_dimension=0, tiled=True
        ).astype(jnp.float32),
        lax.psum_scatter(
            edge_third.astype(jnp.bfloat16), "grp", scatter_dimension=0, tiled=True
        ).astype(jnp.float32),
        lax.psum_scatter(
            edge_gsum.astype(jnp.bfloat16), "grp", scatter_dimension=0, tiled=True
        ).astype(jnp.float32),
        lax.psum_scatter(
            node_first.astype(jnp.bfloat16), "grp", scatter_dimension=0, tiled=True
        ).astype(jnp.float32),
        lax.psum_scatter(
            node_second.astype(jnp.bfloat16), "grp", scatter_dimension=0, tiled=True
        ).astype(jnp.float32),
        lax.psum_scatter(
            node_third.astype(jnp.bfloat16), "grp", scatter_dimension=0, tiled=True
        ).astype(jnp.float32),
        lax.psum_scatter(
            node_gsum.astype(jnp.bfloat16), "grp", scatter_dimension=0, tiled=True
        ).astype(jnp.float32),
    )
    reduced = lax.psum(
        (
            reduced[0],
            reduced[1],
            reduced[2],
            reduced[3],
            reduced[4],
            reduced[5],
            reduced[6],
            reduced[7],
        ),
        "dom",
    )
    arrivals = []
    for direction, offset in enumerate(OFFSETS):
        arrivals.append(from_behind(ghost_grad[direction], "dom", offset))
    arrived = jnp.stack(arrivals)
    node_count = node_total.shape[0]
    targets = recv_index[0].reshape(-1)
    owner_hot = (lax.iota(jnp.int32, node_count)[:, None] == targets[None, :]).astype(jnp.bfloat16)
    node_total = node_total + matmul(owner_hot, arrived.reshape(targets.shape[0], -1))
    grad_node = node_total.astype(jnp.bfloat16)[None]
    partitions = domains * groups
    edge_scale = 1.0 / math.sqrt(partitions * edge_latents.shape[1])
    node_scale = 1.0 / math.sqrt(partitions * node_latents.shape[1])
    return (
        grad_node,
        grad_edge[None],
        reduced[0] * edge_scale,
        reduced[1] * edge_scale,
        reduced[2] * edge_scale,
        reduced[3] * edge_scale,
        reduced[4] * node_scale,
        reduced[5] * node_scale,
        reduced[6] * node_scale,
        reduced[7] * node_scale,
    )


MESH = pl.DeviceIdType.MESH


def one_hot(mask):
    return jnp.where(mask, 1.0, 0.0).astype(jnp.bfloat16)


def hot_pair(ids, count):
    edges = ids.shape[1]
    column = jnp.transpose(jnp.broadcast_to(ids, (128, edges)))
    blocks = []
    for start in range(0, count, 128):
        width = min(128, count - start)
        lane = lax.broadcasted_iota(jnp.int32, (edges, width), 1) + start
        blocks.append(one_hot(column[:, :width] == lane))
    row = lax.broadcasted_iota(jnp.int32, (count, edges), 0)
    return blocks, one_hot(ids == row)


def wide(value):
    return value.astype(jnp.float32)


def narrow(value):
    return value.astype(jnp.bfloat16)


def activate(pre):
    sigma = jax.nn.sigmoid(pre)
    return narrow(pre * sigma), sigma * (1.0 + pre * (1.0 - sigma))


def fused_kernel(
    plan,
    node_lat_hbm,
    ghost_lat_hbm,
    edge_lat_hbm,
    node_cot_hbm,
    edge_cot_hbm,
    senders_hbm,
    receivers_hbm,
    counts_hbm,
    recv_index_hbm,
    ew1_hbm,
    ew2_hbm,
    ew3_hbm,
    egain_hbm,
    nw1_hbm,
    nw2_hbm,
    nw3_hbm,
    ngain_hbm,
    grad_node_hbm,
    grad_edge_hbm,
    out_e1_hbm,
    out_e2_hbm,
    out_e3_hbm,
    out_eg_hbm,
    out_n1_hbm,
    out_n2_hbm,
    out_n3_hbm,
    out_ng_hbm,
    terms_n,
    terms_b,
    terms_c,
    core_n,
    core_b,
    core_c,
    half_n,
    half_b,
    half_c,
    keep_n,
    keep_b,
    keep_c,
    side_n,
    side_b,
    side_c,
    part_n,
    part_b,
    part_c,
    gath_n,
    gath_b,
    gath_c,
    fin_n,
    fin_b,
    fin_c,
    ghost_out,
    ghost_in,
    send_sem,
    recv_sem,
    load_sem,
    node_lat,
    ghost_lat,
    edge_lat,
    node_cot,
    edge_cot,
    senders,
    receivers,
    counts,
    recv_index,
    ew1,
    ew2,
    ew3,
    egain,
    nw1,
    nw2,
    nw3,
    ngain,
    save_sem,
    grad_node,
    grad_edge,
    out_e1,
    out_e2,
    out_e3,
    out_eg,
    out_n1,
    out_n2,
    out_n3,
    out_ng,
):
    saves = [
        pltpu.make_async_copy(staged, target, save_sem.at[number])
        for number, (staged, target) in enumerate(
            (
                (grad_node, grad_node_hbm),
                (grad_edge, grad_edge_hbm),
                (out_e1, out_e1_hbm),
                (out_e2, out_e2_hbm),
                (out_e3, out_e3_hbm),
                (out_eg, out_eg_hbm),
                (out_n1, out_n1_hbm),
                (out_n2, out_n2_hbm),
                (out_n3, out_n3_hbm),
                (out_ng, out_ng_hbm),
            )
        )
    ]
    loads = {}
    for source, staged in (
        (senders_hbm, senders),
        (receivers_hbm, receivers),
        (node_lat_hbm, node_lat),
        (ghost_lat_hbm, ghost_lat),
        (edge_lat_hbm, edge_lat),
        (ew1_hbm, ew1),
        (ew2_hbm, ew2),
        (ew3_hbm, ew3),
        (egain_hbm, egain),
        (nw1_hbm, nw1),
        (nw2_hbm, nw2),
        (nw3_hbm, nw3),
        (node_cot_hbm, node_cot),
        (ngain_hbm, ngain),
        (edge_cot_hbm, edge_cot),
        (counts_hbm, counts),
        (recv_index_hbm, recv_index),
    ):
        load = pltpu.make_async_copy(source, staged, load_sem.at[len(loads)])
        load.start()
        loads[len(loads)] = load

    def need(first, last):
        for number in range(first, last):
            loads[number].wait()

    domains, edge_scale, node_scale = plan
    latent = node_lat.shape[1]
    owned = node_lat.shape[0]
    ghosts = ghost_lat.shape[0]
    slots = ghosts // 4
    blocks = domains // 2
    half = latent // 2
    dom = lax.axis_index("dom")
    grp = lax.axis_index("grp")
    core = lax.rem(grp, 2)
    pair = lax.div(grp, 2)
    other_core = 2 * pair + 1 - core
    other_pair = 2 * (1 - pair) + core
    per_chunk = 2 + 2 * (domains - 1)

    def ahead(step):
        return lax.rem(dom + step + domains, domains)

    barrier = pltpu.get_barrier_semaphore()
    pl.semaphore_signal(barrier, inc=1, device_id={"grp": other_core}, device_id_type=MESH)
    pl.semaphore_signal(barrier, inc=1, device_id={"grp": other_pair}, device_id_type=MESH)
    for step in range(1, domains):
        pl.semaphore_signal(barrier, inc=1, device_id={"dom": ahead(step)}, device_id_type=MESH)

    def remote(src, dst, number, target):
        return pltpu.make_async_remote_copy(
            src_ref=src,
            dst_ref=dst,
            send_sem=send_sem.at[number],
            recv_sem=recv_sem.at[number],
            device_id=target,
            device_id_type=MESH,
        )

    chunks = (
        (terms_n, core_n, half_n, keep_n, side_n, part_n, gath_n, fin_n),
        (terms_b, core_b, half_b, keep_b, side_b, part_b, gath_b, fin_b),
        (terms_c, core_c, half_c, keep_c, side_c, part_c, gath_c, fin_c),
    )

    def put(number, matrices, tail=None):
        terms = chunks[number][0]
        for quarter in range(4):
            rows = []
            for matrix in matrices:
                share = matrix.shape[0] // 4
                rows.append(matrix[quarter * share : (quarter + 1) * share])
            rows = narrow(rows[0] if len(rows) == 1 else jnp.concatenate(rows, axis=0))
            size = rows.shape[0] // blocks
            for piece in range(domains):
                at = (piece // 2) * size
                lane = (piece % 2) * half
                terms[quarter % 2, quarter // 2, piece, 0:size] = rows[
                    at : at + size, lane : lane + half
                ]
                if tail is not None:
                    terms[quarter % 2, quarter // 2, piece, size : size + 16] = tail

    def over_core(number):
        terms, arrived = chunks[number][0:2]
        return remote(
            terms.at[1 - core], arrived, number * per_chunk, {"grp": other_core}
        )

    def over_pair(number):
        return remote(
            chunks[number][2], chunks[number][4], number * per_chunk + 1, {"grp": other_pair}
        )

    def over_dom(number):
        part, gath = chunks[number][5:7]
        return [
            remote(
                part.at[ahead(step)],
                gath.at[step],
                number * per_chunk + 1 + step,
                {"dom": ahead(step)},
            )
            for step in range(1, domains)
        ]

    def spread(number):
        fin = chunks[number][7]
        return [
            remote(
                fin.at[0],
                fin.at[step],
                number * per_chunk + domains + step,
                {"dom": ahead(step)},
            )
            for step in range(1, domains)
        ]

    def stage_pair(number):
        terms, arrived, send, keep = chunks[number][0:4]
        over_core(number).wait()
        send[...] = narrow(wide(terms[core, 1 - pair]) + wide(arrived[1 - pair]))
        over_pair(number).start()
        keep[...] = wide(terms[core, pair]) + wide(arrived[pair])

    def stage_dom(number):
        keep, side, part = chunks[number][3:6]
        over_pair(number).wait()
        part[...] = narrow(keep[...] + wide(side[...]))
        for copy in over_dom(number):
            copy.start()

    def stage_spread(number):
        part, gath, fin = chunks[number][5:8]
        for copy in over_dom(number):
            copy.wait()
        total = wide(part[dom])
        for step in range(1, domains):
            total = total + wide(gath[step])
        fin[0] = narrow(total[: fin.shape[1]])
        for copy in spread(number):
            copy.start()
        return total

    def stage_out(number, outs, scale):
        fin = chunks[number][7]
        for copy in spread(number):
            copy.wait()
        size = fin.shape[1]
        for piece in range(domains):
            value = wide(fin[lax.rem(dom - piece + domains, domains)]) * scale
            lane = (piece % 2) * half
            first = (piece // 2) * size
            base = 0
            for out in outs:
                low, high = max(first, base), min(first + size, base + out.shape[0])
                if low < high:
                    out[low - base : high - base, lane : lane + half] = value[
                        low - first : high - first
                    ]
                base += out.shape[0]

    need(0, 2)
    sender_blocks, sender_rows = hot_pair(senders[...], owned + ghosts)
    receiver_blocks, receiver_rows = hot_pair(receivers[...], owned)
    receiver_hot = jnp.concatenate(receiver_blocks, axis=1)
    node_blocks = owned // 128
    sender_hot = jnp.concatenate(sender_blocks[:node_blocks], axis=1)
    ghost_hot = jnp.concatenate(sender_blocks[node_blocks:], axis=1)
    need(2, 5)
    own_lat = node_lat[...]
    edge_in0 = edge_lat[...]
    edge_in1 = narrow(matmul(sender_hot, own_lat) + matmul(ghost_hot, ghost_lat[...]))
    edge_in2 = narrow(matmul(receiver_hot, own_lat))

    need(5, 9)
    pre = (
        matmul(edge_in0, ew1[0:latent])
        + matmul(edge_in1, ew1[latent : 2 * latent])
        + matmul(edge_in2, ew1[2 * latent : 3 * latent])
    )
    e_act1, e_slope1 = activate(pre)
    e_act2, e_slope2 = activate(matmul(e_act1, ew2[...]))
    e_normed, e_norm = norm_parts(matmul(e_act2, ew3[...]))
    updated = narrow(wide(edge_in0) + e_normed * egain[...])
    summed = narrow(matmul(receiver_rows, updated))

    need(9, 17)
    pre = matmul(own_lat, nw1[0:latent]) + matmul(summed, nw1[latent : 2 * latent])
    n_act1, n_slope1 = activate(pre)
    n_act2, n_slope2 = activate(matmul(n_act1, nw2[...]))
    n_normed, n_norm = norm_parts(matmul(n_act2, nw3[...]))
    node_up = wide(node_cot[...])
    n_gsum = jnp.sum(node_up * n_normed, axis=0, keepdims=True)
    q3 = narrow(norm_back(node_up * ngain[...], n_normed, n_norm))
    q2 = narrow(against(q3, nw3[...]) * n_slope2)
    q1 = narrow(against(q2, nw2[...]) * n_slope1)
    back_summed = narrow(against(q1, nw1[latent : 2 * latent]))
    put(
        0,
        (
            jnp.concatenate([over_rows(own_lat, q1), over_rows(summed, q1)], axis=0),
            over_rows(n_act1, q2),
            over_rows(n_act2, q3),
        ),
    )
    pl.semaphore_wait(barrier, domains + 1)
    over_core(0).start()

    node_part = node_up + against(q1, nw1[0:latent])
    edge_up = wide(edge_cot[...]) + matmul(receiver_hot, back_summed)
    e_gsum = jnp.sum(edge_up * e_normed, axis=0, keepdims=True)
    q3 = narrow(norm_back(edge_up * egain[...], e_normed, e_norm))
    stage_pair(0)
    q2 = narrow(against(q3, ew3[...]) * e_slope2)
    row = lax.broadcasted_iota(jnp.int32, (16, half), 0)
    tail = jnp.where(row == 0, e_gsum[:, :half], 0.0)
    tail = jnp.where(row == 1, e_gsum[:, half:], tail)
    tail = jnp.where(row == 2, n_gsum[:, :half], tail)
    tail = narrow(jnp.where(row == 3, n_gsum[:, half:], tail))
    put(1, (over_rows(e_act1, q2), over_rows(e_act2, q3)), tail)
    over_core(1).start()
    q1 = narrow(against(q2, ew2[...]) * e_slope1)
    stage_dom(0)
    put(
        2,
        (
            jnp.concatenate(
                [over_rows(edge_in0, q1), over_rows(edge_in1, q1), over_rows(edge_in2, q1)],
                axis=0,
            ),
        ),
    )
    over_core(2).start()
    stage_pair(1)

    to_sender = narrow(against(q1, ew1[latent : 2 * latent]))
    to_table = matmul(sender_rows, to_sender)
    slot = lax.broadcasted_iota(jnp.int32, (slots, latent), 0)
    halos = []
    for direction, offset in enumerate(OFFSETS):
        first = owned + direction * slots
        live = slot < counts[:, direction : direction + 1]
        ghost_out[direction] = narrow(jnp.where(live, to_table[first : first + slots], 0.0))
        halo = remote(
            ghost_out.at[direction],
            ghost_in.at[direction],
            3 * per_chunk + direction,
            {"dom": ahead(offset)},
        )
        halo.start()
        halos.append(halo)
    stage_pair(2)
    stage_dom(1)
    to_receiver = narrow(against(q1, ew1[2 * latent : 3 * latent]))
    node_part = node_part + to_table[:owned] + matmul(receiver_rows, to_receiver)
    stage_spread(0)
    stage_dom(2)
    grad_edge[...] = narrow(edge_up + against(q1, ew1[0:latent]))
    saves[1].start()
    gains = stage_spread(1)
    gains = gains[gains.shape[0] - 16 :]
    quarter = latent // 4
    for out, first, scale in ((out_eg, 0, edge_scale), (out_ng, 2, node_scale)):
        line = jnp.where(pair == 0, gains[first : first + 1], gains[first + 1 : first + 2])
        out[...] = jnp.where(core == 0, line[:, :quarter], line[:, quarter:]) * scale
    for halo in halos:
        halo.wait()
    owner = lax.broadcasted_iota(jnp.int32, (owned, slots), 0)
    for direction in range(4):
        hot = one_hot(owner == recv_index[direction : direction + 1, :])
        node_part = node_part + matmul(hot, ghost_in[direction])
    grad_node[...] = narrow(node_part)
    for number in (0, 5, 9):
        saves[number].start()
    stage_spread(2)
    stage_out(0, (out_n1, out_n2, out_n3), node_scale)
    for number in (6, 7, 8):
        saves[number].start()
    stage_out(1, (out_e2, out_e3), edge_scale)
    for number in (3, 4):
        saves[number].start()
    stage_out(2, (out_e1,), edge_scale)
    saves[2].start()
    for save in saves:
        save.wait()


def store_kernel(*refs):
    ins, outs, held = refs[:10], refs[10:20], refs[20:30]
    load_sem, store_sem = refs[30:]
    loads = [pltpu.make_async_copy(ins[at], held[at], load_sem.at[at]) for at in range(10)]
    stores = [pltpu.make_async_copy(held[at], outs[at], store_sem.at[at]) for at in range(10)]
    for load in loads:
        load.start()
    for load, store in zip(loads, stores):
        load.wait()
        store.start()
    for store in stores:
        store.wait()


def fused_device(
    node_latents,
    ghost_latents,
    edge_latents,
    node_cotangent,
    edge_cotangent,
    senders,
    receivers,
    halo_counts,
    recv_index,
    edge_w1,
    edge_w2,
    edge_w3,
    edge_gain,
    node_w1,
    node_w2,
    node_w3,
    node_gain,
):
    domains = lax.axis_size("dom")
    groups = lax.axis_size("grp")
    nodes, latent = node_latents.shape[1:]
    edges = edge_latents.shape[1]
    slots = ghost_latents.shape[1] // 4
    partitions = domains * groups
    plan = (
        domains,
        1.0 / math.sqrt(partitions * edges),
        1.0 / math.sqrt(partitions * nodes),
    )
    half = latent // 2
    quarter = latent // 4
    blocks = domains // 2
    bulk = [
        node_w1.shape[0] // 4 + 2 * quarter,
        2 * quarter,
        edge_w1.shape[0] // 4,
    ]
    clean = [rows // blocks for rows in bulk]
    sizes = [clean[0], clean[1] + 16, clean[2]]

    def buffers(lead, kind, rows=sizes):
        return [pltpu.VMEM((*lead, size, half), kind) for size in rows]

    scratch = (
        buffers((2, 2, domains), jnp.bfloat16)
        + buffers((2, domains), jnp.bfloat16)
        + buffers((domains,), jnp.bfloat16)
        + buffers((domains,), jnp.float32)
        + buffers((domains,), jnp.bfloat16)
        + buffers((domains,), jnp.bfloat16)
        + buffers((domains,), jnp.bfloat16)
        + buffers((domains,), jnp.bfloat16, clean)
        + [
            pltpu.VMEM((4, slots, latent), jnp.bfloat16),
            pltpu.VMEM((4, slots, latent), jnp.bfloat16),
        ]
    )
    copies = 3 * (2 + 2 * (domains - 1)) + 4
    scratch += [pltpu.SemaphoreType.DMA((copies,)), pltpu.SemaphoreType.DMA((copies,))]
    operands = (
        node_latents[0],
        ghost_latents[0],
        edge_latents[0],
        node_cotangent[0],
        edge_cotangent[0],
        senders,
        receivers,
        halo_counts,
        recv_index[0],
        edge_w1,
        edge_w2,
        edge_w3,
        edge_gain[None],
        node_w1,
        node_w2,
        node_w3,
        node_gain[None],
    )
    scratch += [pltpu.SemaphoreType.DMA((len(operands),))]
    scratch += [pltpu.VMEM(operand.shape, operand.dtype) for operand in operands]

    def grad(rows):
        return jax.ShapeDtypeStruct((rows, latent), jnp.float32)

    gain = jax.ShapeDtypeStruct((1, quarter), jnp.float32)
    shapes = (
        jax.ShapeDtypeStruct((nodes, latent), jnp.bfloat16),
        jax.ShapeDtypeStruct((edges, latent), jnp.bfloat16),
        grad(edge_w1.shape[0] // 4),
        grad(quarter),
        grad(quarter),
        gain,
        grad(node_w1.shape[0] // 4),
        grad(quarter),
        grad(quarter),
        gain,
    )
    scratch += [pltpu.SemaphoreType.DMA((len(shapes),))]
    scratch += [pltpu.VMEM(out.shape, out.dtype) for out in shapes]
    outs = pl.pallas_call(
        functools.partial(fused_kernel, plan),
        out_shape=shapes,
        in_specs=[pl.BlockSpec(memory_space=pltpu.HBM)] * len(operands),
        out_specs=[pl.BlockSpec(memory_space=pltpu.HBM)] * 10,
        scratch_shapes=scratch,
        compiler_params=pltpu.CompilerParams(
            collective_id=0, has_side_effects=True, vmem_limit_bytes=60 * 1024 * 1024
        ),
    )(*operands)
    outs = pl.pallas_call(
        store_kernel,
        out_shape=tuple(jax.ShapeDtypeStruct(out.shape, out.dtype) for out in outs),
        in_specs=[pl.BlockSpec(memory_space=pltpu.HBM)] * 10,
        out_specs=[pl.BlockSpec(memory_space=pltpu.HBM)] * 10,
        scratch_shapes=[pltpu.VMEM(out.shape, out.dtype) for out in outs]
        + [pltpu.SemaphoreType.DMA((10,)), pltpu.SemaphoreType.DMA((10,))],
        compiler_params=pltpu.CompilerParams(vmem_limit_bytes=60 * 1024 * 1024),
    )(*outs)
    outs = list(outs)
    outs[0] = outs[0][None]
    outs[1] = outs[1][None]
    outs[5] = outs[5][0]
    outs[9] = outs[9][0]
    return tuple(outs)


def solution(mesh):
    placed = (
        P("grp", "dom", None),
        P("grp", "dom", None),
        P("grp", "dom", None),
        P("grp", "dom", None),
        P("grp", "dom", None),
        P("grp", "dom"),
        P("grp", "dom"),
        P("grp", "dom"),
        P("grp", "dom", None),
        P(),
        P(),
        P(),
        P(),
        P(),
        P(),
        P(),
        P(),
    )
    domains, groups = mesh.shape["dom"], mesh.shape["grp"]
    fits = groups == 4 and domains == 8
    return jax.shard_map(
        fused_device if fits else per_device,
        mesh=mesh,
        in_specs=placed,
        out_specs=(
            P("grp", "dom", None),
            P("grp", "dom", None),
            P("grp", None),
            P("grp", None),
            P("grp", None),
            P("grp"),
            P("grp", None),
            P("grp", None),
            P("grp", None),
            P("grp"),
        ),
        check_vma=False,
    )
```

```python
import functools
import math

import jax
import jax.numpy as jnp
from jax import lax
from jax.experimental import pallas as pl
from jax.experimental.pallas import tpu as pltpu
from jax.sharding import PartitionSpec as P

EPS = 1e-05
OFFSETS = (-2, -1, 1, 2)


def from_behind(block, axis, distance):
    devices = range(lax.axis_size(axis))
    route = [(i - distance, i) for i in devices if i - distance in devices]
    return lax.ppermute(block, axis, route)


def matmul(left, right):
    return jnp.dot(left, right, preferred_element_type=jnp.float32)


def over_rows(left, right):
    return lax.dot_general(
        left, right, (((0,), (0,)), ((), ())), preferred_element_type=jnp.float32
    )


def against(left, weight):
    return lax.dot_general(
        left, weight, (((1,), (1,)), ((), ())), preferred_element_type=jnp.float32
    )


def silu_slope(value):
    sigma = jax.nn.sigmoid(value)
    return sigma * (1.0 + value * (1.0 - sigma))


def norm_parts(value):
    centre = value - jnp.mean(value, axis=-1, keepdims=True)
    scale = lax.rsqrt(jnp.mean(centre * centre, axis=-1, keepdims=True) + EPS)
    return (centre * scale, scale)


def norm_back(upstream, normed, scale):
    return scale * (
        upstream
        - jnp.mean(upstream, axis=-1, keepdims=True)
        - normed * jnp.mean(upstream * normed, axis=-1, keepdims=True)
    )


def mlp_forward(inputs, first_w, second_w, third_w, gain):
    pre_one = matmul(inputs, first_w)
    act_one = jax.nn.silu(pre_one).astype(jnp.bfloat16)
    pre_two = matmul(act_one, second_w)
    act_two = jax.nn.silu(pre_two).astype(jnp.bfloat16)
    normed, scale = norm_parts(matmul(act_two, third_w))
    return (normed * gain, (pre_one, act_one, pre_two, act_two, normed, scale))


def mlp_backward(inputs, first_w, second_w, third_w, gain, saved, upstream):
    pre_one, act_one, pre_two, act_two, normed, scale = saved
    grad_gain = jnp.sum(upstream * normed, axis=0)
    delta_out = norm_back(upstream * gain, normed, scale).astype(jnp.bfloat16)
    grad_third = over_rows(act_two, delta_out)
    delta_two = (against(delta_out, third_w) * silu_slope(pre_two)).astype(jnp.bfloat16)
    grad_second = over_rows(act_one, delta_two)
    delta_one = (against(delta_two, second_w) * silu_slope(pre_one)).astype(jnp.bfloat16)
    grad_first = over_rows(inputs, delta_one)
    return (against(delta_one, first_w), (grad_first, grad_second, grad_third, grad_gain))


def local_pass(
    node_lat, ghost_lat, edge_lat, node_cot, edge_cot, sender_ids, receiver_ids, counts, weights
):
    edge_one, edge_two, edge_three, edge_g, node_one, node_two, node_three, node_g = weights
    node_count = node_lat.shape[0]
    ghost_count = ghost_lat.shape[0]
    slot_count = ghost_count // 4
    latent = node_lat.shape[1]
    node_table = jnp.concatenate([node_lat, ghost_lat], axis=0)
    send_hot = (
        sender_ids[:, None] == lax.iota(jnp.int32, node_count + ghost_count)[None, :]
    ).astype(jnp.bfloat16)
    recv_hot = (receiver_ids[:, None] == lax.iota(jnp.int32, node_count)[None, :]).astype(
        jnp.bfloat16
    )
    sender_lat = matmul(send_hot, node_table).astype(jnp.bfloat16)
    receiver_lat = matmul(recv_hot, node_lat).astype(jnp.bfloat16)
    edge_in = jnp.concatenate([edge_lat, sender_lat, receiver_lat], axis=1)
    message, edge_saved = mlp_forward(edge_in, edge_one, edge_two, edge_three, edge_g)
    updated = (edge_lat.astype(jnp.float32) + message).astype(jnp.bfloat16)
    summed = over_rows(recv_hot, updated).astype(jnp.bfloat16)
    node_in = jnp.concatenate([node_lat, summed], axis=1)
    unused_out, node_saved = mlp_forward(node_in, node_one, node_two, node_three, node_g)
    node_up = node_cot.astype(jnp.float32)
    node_grad_in, node_terms = mlp_backward(
        node_in, node_one, node_two, node_three, node_g, node_saved, node_up
    )
    back_summed = node_grad_in[:, latent:].astype(jnp.bfloat16)
    edge_up = edge_cot.astype(jnp.float32) + matmul(recv_hot, back_summed)
    edge_grad_in, edge_terms = mlp_backward(
        edge_in, edge_one, edge_two, edge_three, edge_g, edge_saved, edge_up
    )
    grad_edge = (edge_up + edge_grad_in[:, :latent]).astype(jnp.bfloat16)
    to_sender = edge_grad_in[:, latent : 2 * latent].astype(jnp.bfloat16)
    to_receiver = edge_grad_in[:, 2 * latent :].astype(jnp.bfloat16)
    to_table = over_rows(send_hot, to_sender)
    node_total = (
        node_up
        + node_grad_in[:, :latent]
        + over_rows(recv_hot, to_receiver)
        + to_table[:node_count]
    )
    ghost_grad = to_table[node_count:].reshape(4, slot_count, latent)
    is_live = lax.iota(jnp.int32, slot_count)[None, :] < counts[:, None]
    ghost_grad = jnp.where(is_live[:, :, None], ghost_grad, 0.0).astype(jnp.bfloat16)
    return (grad_edge, node_total, ghost_grad, edge_terms + node_terms)


def per_device(
    node_latents,
    ghost_latents,
    edge_latents,
    node_cotangent,
    edge_cotangent,
    senders,
    receivers,
    halo_counts,
    recv_index,
    edge_w1,
    edge_w2,
    edge_w3,
    edge_gain,
    node_w1,
    node_w2,
    node_w3,
    node_gain,
):
    weights = (edge_w1, edge_w2, edge_w3, edge_gain, node_w1, node_w2, node_w3, node_gain)
    grad_edge, node_total, ghost_grad, grad_terms = local_pass(
        node_latents[0],
        ghost_latents[0],
        edge_latents[0],
        node_cotangent[0],
        edge_cotangent[0],
        senders[0],
        receivers[0],
        halo_counts[0],
        weights,
    )
    (
        edge_first,
        edge_second,
        edge_third,
        edge_gsum,
        node_first,
        node_second,
        node_third,
        node_gsum,
    ) = grad_terms
    domains = lax.axis_size("dom")
    groups = lax.axis_size("grp")
    reduced = (
        lax.psum_scatter(
            edge_first.astype(jnp.bfloat16), "grp", scatter_dimension=0, tiled=True
        ).astype(jnp.float32),
        lax.psum_scatter(
            edge_second.astype(jnp.bfloat16), "grp", scatter_dimension=0, tiled=True
        ).astype(jnp.float32),
        lax.psum_scatter(
            edge_third.astype(jnp.bfloat16), "grp", scatter_dimension=0, tiled=True
        ).astype(jnp.float32),
        lax.psum_scatter(
            edge_gsum.astype(jnp.bfloat16), "grp", scatter_dimension=0, tiled=True
        ).astype(jnp.float32),
        lax.psum_scatter(
            node_first.astype(jnp.bfloat16), "grp", scatter_dimension=0, tiled=True
        ).astype(jnp.float32),
        lax.psum_scatter(
            node_second.astype(jnp.bfloat16), "grp", scatter_dimension=0, tiled=True
        ).astype(jnp.float32),
        lax.psum_scatter(
            node_third.astype(jnp.bfloat16), "grp", scatter_dimension=0, tiled=True
        ).astype(jnp.float32),
        lax.psum_scatter(
            node_gsum.astype(jnp.bfloat16), "grp", scatter_dimension=0, tiled=True
        ).astype(jnp.float32),
    )
    reduced = lax.psum(
        (
            reduced[0],
            reduced[1],
            reduced[2],
            reduced[3],
            reduced[4],
            reduced[5],
            reduced[6],
            reduced[7],
        ),
        "dom",
    )
    arrivals = []
    for direction, offset in enumerate(OFFSETS):
        arrivals.append(from_behind(ghost_grad[direction], "dom", offset))
    arrived = jnp.stack(arrivals)
    node_count = node_total.shape[0]
    targets = recv_index[0].reshape(-1)
    owner_hot = (lax.iota(jnp.int32, node_count)[:, None] == targets[None, :]).astype(jnp.bfloat16)
    node_total = node_total + matmul(owner_hot, arrived.reshape(targets.shape[0], -1))
    grad_node = node_total.astype(jnp.bfloat16)[None]
    partitions = domains * groups
    edge_scale = 1.0 / math.sqrt(partitions * edge_latents.shape[1])
    node_scale = 1.0 / math.sqrt(partitions * node_latents.shape[1])
    return (
        grad_node,
        grad_edge[None],
        reduced[0] * edge_scale,
        reduced[1] * edge_scale,
        reduced[2] * edge_scale,
        reduced[3] * edge_scale,
        reduced[4] * node_scale,
        reduced[5] * node_scale,
        reduced[6] * node_scale,
        reduced[7] * node_scale,
    )


MESH = pl.DeviceIdType.MESH


def one_hot(mask):
    return jnp.where(mask, 1.0, 0.0).astype(jnp.bfloat16)


def hot_pair(ids, count):
    edges = ids.shape[1]
    column = jnp.transpose(jnp.broadcast_to(ids, (128, edges)))
    blocks = []
    for start in range(0, count, 128):
        width = min(128, count - start)
        lane = lax.broadcasted_iota(jnp.int32, (edges, width), 1) + start
        blocks.append(one_hot(column[:, :width] == lane))
    row = lax.broadcasted_iota(jnp.int32, (count, edges), 0)
    return blocks, one_hot(ids == row)


def wide(value):
    return value.astype(jnp.float32)


def narrow(value):
    return value.astype(jnp.bfloat16)


def activate(pre):
    sigma = jax.nn.sigmoid(pre)
    return narrow(pre * sigma), sigma * (1.0 + pre * (1.0 - sigma))


def fused_kernel(
    plan,
    node_lat_hbm,
    ghost_lat_hbm,
    edge_lat_hbm,
    node_cot_hbm,
    edge_cot_hbm,
    senders_hbm,
    receivers_hbm,
    counts_hbm,
    recv_index_hbm,
    ew1_hbm,
    ew2_hbm,
    ew3_hbm,
    egain_hbm,
    nw1_hbm,
    nw2_hbm,
    nw3_hbm,
    ngain_hbm,
    grad_node_hbm,
    grad_edge_hbm,
    out_e1_hbm,
    out_e2_hbm,
    out_e3_hbm,
    out_eg_hbm,
    out_n1_hbm,
    out_n2_hbm,
    out_n3_hbm,
    out_ng_hbm,
    terms_n,
    terms_b,
    terms_c,
    core_n,
    core_b,
    core_c,
    half_n,
    half_b,
    half_c,
    keep_n,
    keep_b,
    keep_c,
    side_n,
    side_b,
    side_c,
    part_n,
    part_b,
    part_c,
    gath_n,
    gath_b,
    gath_c,
    fin_n,
    fin_b,
    fin_c,
    ghost_out,
    ghost_in,
    send_sem,
    recv_sem,
    load_sem,
    node_lat,
    ghost_lat,
    edge_lat,
    node_cot,
    edge_cot,
    senders,
    receivers,
    counts,
    recv_index,
    ew1,
    ew2,
    ew3,
    egain,
    nw1,
    nw2,
    nw3,
    ngain,
    save_sem,
    grad_node,
    grad_edge,
    out_e1,
    out_e2,
    out_e3,
    out_eg,
    out_n1,
    out_n2,
    out_n3,
    out_ng,
):
    saves = [
        pltpu.make_async_copy(staged, target, save_sem.at[number])
        for number, (staged, target) in enumerate(
            (
                (grad_node, grad_node_hbm),
                (grad_edge, grad_edge_hbm),
                (out_e1, out_e1_hbm),
                (out_e2, out_e2_hbm),
                (out_e3, out_e3_hbm),
                (out_eg, out_eg_hbm),
                (out_n1, out_n1_hbm),
                (out_n2, out_n2_hbm),
                (out_n3, out_n3_hbm),
                (out_ng, out_ng_hbm),
            )
        )
    ]
    loads = {}
    for source, staged in (
        (senders_hbm, senders),
        (receivers_hbm, receivers),
        (node_lat_hbm, node_lat),
        (ghost_lat_hbm, ghost_lat),
        (edge_lat_hbm, edge_lat),
        (ew1_hbm, ew1),
        (ew2_hbm, ew2),
        (ew3_hbm, ew3),
        (egain_hbm, egain),
        (nw1_hbm, nw1),
        (nw2_hbm, nw2),
        (nw3_hbm, nw3),
        (node_cot_hbm, node_cot),
        (ngain_hbm, ngain),
        (edge_cot_hbm, edge_cot),
        (counts_hbm, counts),
        (recv_index_hbm, recv_index),
    ):
        load = pltpu.make_async_copy(source, staged, load_sem.at[len(loads)])
        load.start()
        loads[len(loads)] = load

    def need(first, last):
        for number in range(first, last):
            loads[number].wait()

    domains, edge_scale, node_scale = plan
    latent = node_lat.shape[1]
    owned = node_lat.shape[0]
    ghosts = ghost_lat.shape[0]
    slots = ghosts // 4
    blocks = domains // 2
    half = latent // 2
    dom = lax.axis_index("dom")
    grp = lax.axis_index("grp")
    core = lax.rem(grp, 2)
    pair = lax.div(grp, 2)
    other_core = 2 * pair + 1 - core
    other_pair = 2 * (1 - pair) + core
    per_chunk = 2 + 2 * (domains - 1)

    def ahead(step):
        return lax.rem(dom + step + domains, domains)

    barrier = pltpu.get_barrier_semaphore()
    pl.semaphore_signal(barrier, inc=1, device_id={"grp": other_core}, device_id_type=MESH)
    pl.semaphore_signal(barrier, inc=1, device_id={"grp": other_pair}, device_id_type=MESH)
    for step in range(1, domains):
        pl.semaphore_signal(barrier, inc=1, device_id={"dom": ahead(step)}, device_id_type=MESH)

    def remote(src, dst, number, target):
        return pltpu.make_async_remote_copy(
            src_ref=src,
            dst_ref=dst,
            send_sem=send_sem.at[number],
            recv_sem=recv_sem.at[number],
            device_id=target,
            device_id_type=MESH,
        )

    chunks = (
        (terms_n, core_n, half_n, keep_n, side_n, part_n, gath_n, fin_n),
        (terms_b, core_b, half_b, keep_b, side_b, part_b, gath_b, fin_b),
        (terms_c, core_c, half_c, keep_c, side_c, part_c, gath_c, fin_c),
    )

    def put(number, matrices, tail=None):
        terms = chunks[number][0]
        for quarter in range(4):
            rows = []
            for matrix in matrices:
                share = matrix.shape[0] // 4
                rows.append(matrix[quarter * share : (quarter + 1) * share])
            rows = narrow(rows[0] if len(rows) == 1 else jnp.concatenate(rows, axis=0))
            size = rows.shape[0] // blocks
            for piece in range(domains):
                at = (piece // 2) * size
                lane = (piece % 2) * half
                terms[quarter % 2, quarter // 2, piece, 0:size] = rows[
                    at : at + size, lane : lane + half
                ]
                if tail is not None:
                    terms[quarter % 2, quarter // 2, piece, size : size + 16] = tail

    def over_core(number):
        terms, arrived = chunks[number][0:2]
        return remote(
            terms.at[1 - core], arrived, number * per_chunk, {"grp": other_core}
        )

    def over_pair(number):
        return remote(
            chunks[number][2], chunks[number][4], number * per_chunk + 1, {"grp": other_pair}
        )

    def over_dom(number):
        part, gath = chunks[number][5:7]
        return [
            remote(
                part.at[ahead(step)],
                gath.at[step],
                number * per_chunk + 1 + step,
                {"dom": ahead(step)},
            )
            for step in range(1, domains)
        ]

    column = lax.rem(dom, 2)
    line = lax.div(dom, 2)

    def across(number):
        fin = chunks[number][7]
        return remote(
            fin.at[pl.ds(0, blocks)],
            fin.at[pl.ds(blocks, blocks)],
            number * per_chunk + domains + blocks,
            {"dom": dom + 1 - 2 * column},
        )

    def stage_across(number):
        for copy in spread(number):
            copy.wait()
        across(number).start()

    def spread(number):
        fin = chunks[number][7]
        if number < 2:
            return [
                remote(
                    fin.at[0],
                    fin.at[step],
                    number * per_chunk + domains + step,
                    {"dom": ahead(2 * step)},
                )
                for step in range(1, blocks)
            ]
        return [
            remote(
                fin.at[0],
                fin.at[step],
                number * per_chunk + domains + step,
                {"dom": ahead(step)},
            )
            for step in range(1, domains)
        ]

    def stage_pair(number):
        terms, arrived, send, keep = chunks[number][0:4]
        over_core(number).wait()
        send[...] = narrow(wide(terms[core, 1 - pair]) + wide(arrived[1 - pair]))
        over_pair(number).start()
        keep[...] = wide(terms[core, pair]) + wide(arrived[pair])

    def stage_dom(number):
        keep, side, part = chunks[number][3:6]
        over_pair(number).wait()
        part[...] = narrow(keep[...] + wide(side[...]))
        for copy in over_dom(number):
            copy.start()

    def stage_spread(number):
        part, gath, fin = chunks[number][5:8]
        for copy in over_dom(number):
            copy.wait()
        total = wide(part[dom])
        for step in range(1, domains):
            total = total + wide(gath[step])
        fin[0] = narrow(total[: fin.shape[1]])
        for copy in spread(number):
            copy.start()
        return total

    def stage_out(number, outs, scale):
        fin = chunks[number][7]
        for copy in [across(number)] if number < 2 else spread(number):
            copy.wait()
        size = fin.shape[1]
        for piece in range(domains):
            slot = lax.rem(dom - piece + domains, domains)
            if number < 2:
                turn = lax.rem(column + piece, 2)
                slot = turn * blocks + lax.rem(line - piece // 2 + blocks, blocks)
            value = wide(fin[slot]) * scale
            lane = (piece % 2) * half
            first = (piece // 2) * size
            base = 0
            for out in outs:
                low, high = max(first, base), min(first + size, base + out.shape[0])
                if low < high:
                    out[low - base : high - base, lane : lane + half] = value[
                        low - first : high - first
                    ]
                base += out.shape[0]

    need(0, 2)
    sender_blocks, sender_rows = hot_pair(senders[...], owned + ghosts)
    receiver_blocks, receiver_rows = hot_pair(receivers[...], owned)
    receiver_hot = jnp.concatenate(receiver_blocks, axis=1)
    node_blocks = owned // 128
    sender_hot = jnp.concatenate(sender_blocks[:node_blocks], axis=1)
    ghost_hot = jnp.concatenate(sender_blocks[node_blocks:], axis=1)
    need(2, 5)
    own_lat = node_lat[...]
    edge_in0 = edge_lat[...]
    edge_in1 = narrow(matmul(sender_hot, own_lat) + matmul(ghost_hot, ghost_lat[...]))
    edge_in2 = narrow(matmul(receiver_hot, own_lat))

    need(5, 9)
    pre = (
        matmul(edge_in0, ew1[0:latent])
        + matmul(edge_in1, ew1[latent : 2 * latent])
        + matmul(edge_in2, ew1[2 * latent : 3 * latent])
    )
    e_act1, e_slope1 = activate(pre)
    e_act2, e_slope2 = activate(matmul(e_act1, ew2[...]))
    e_normed, e_norm = norm_parts(matmul(e_act2, ew3[...]))
    updated = narrow(wide(edge_in0) + e_normed * egain[...])
    summed = narrow(matmul(receiver_rows, updated))

    need(9, 17)
    pre = matmul(own_lat, nw1[0:latent]) + matmul(summed, nw1[latent : 2 * latent])
    n_act1, n_slope1 = activate(pre)
    n_act2, n_slope2 = activate(matmul(n_act1, nw2[...]))
    n_normed, n_norm = norm_parts(matmul(n_act2, nw3[...]))
    node_up = wide(node_cot[...])
    n_gsum = jnp.sum(node_up * n_normed, axis=0, keepdims=True)
    q3 = narrow(norm_back(node_up * ngain[...], n_normed, n_norm))
    q2 = narrow(against(q3, nw3[...]) * n_slope2)
    q1 = narrow(against(q2, nw2[...]) * n_slope1)
    back_summed = narrow(against(q1, nw1[latent : 2 * latent]))
    put(
        0,
        (
            jnp.concatenate([over_rows(own_lat, q1), over_rows(summed, q1)], axis=0),
            over_rows(n_act1, q2),
            over_rows(n_act2, q3),
        ),
    )
    pl.semaphore_wait(barrier, domains + 1)
    over_core(0).start()

    node_part = node_up + against(q1, nw1[0:latent])
    edge_up = wide(edge_cot[...]) + matmul(receiver_hot, back_summed)
    e_gsum = jnp.sum(edge_up * e_normed, axis=0, keepdims=True)
    q3 = narrow(norm_back(edge_up * egain[...], e_normed, e_norm))
    stage_pair(0)
    q2 = narrow(against(q3, ew3[...]) * e_slope2)
    row = lax.broadcasted_iota(jnp.int32, (16, half), 0)
    tail = jnp.where(row == 0, e_gsum[:, :half], 0.0)
    tail = jnp.where(row == 1, e_gsum[:, half:], tail)
    tail = jnp.where(row == 2, n_gsum[:, :half], tail)
    tail = narrow(jnp.where(row == 3, n_gsum[:, half:], tail))
    put(1, (over_rows(e_act1, q2), over_rows(e_act2, q3)), tail)
    over_core(1).start()
    q1 = narrow(against(q2, ew2[...]) * e_slope1)
    stage_dom(0)
    put(
        2,
        (
            jnp.concatenate(
                [over_rows(edge_in0, q1), over_rows(edge_in1, q1), over_rows(edge_in2, q1)],
                axis=0,
            ),
        ),
    )
    over_core(2).start()
    stage_pair(1)

    to_sender = narrow(against(q1, ew1[latent : 2 * latent]))
    to_table = matmul(sender_rows, to_sender)
    slot = lax.broadcasted_iota(jnp.int32, (slots, latent), 0)
    halos = []
    for direction, offset in enumerate(OFFSETS):
        first = owned + direction * slots
        live = slot < counts[:, direction : direction + 1]
        ghost_out[direction] = narrow(jnp.where(live, to_table[first : first + slots], 0.0))
        halo = remote(
            ghost_out.at[direction],
            ghost_in.at[direction],
            3 * per_chunk + direction,
            {"dom": ahead(offset)},
        )
        halo.start()
        halos.append(halo)
    stage_pair(2)
    stage_dom(1)
    to_receiver = narrow(against(q1, ew1[2 * latent : 3 * latent]))
    node_part = node_part + to_table[:owned] + matmul(receiver_rows, to_receiver)
    stage_spread(0)
    stage_dom(2)
    grad_edge[...] = narrow(edge_up + against(q1, ew1[0:latent]))
    saves[1].start()
    gains = stage_spread(1)
    gains = gains[gains.shape[0] - 16 :]
    quarter = latent // 4
    for out, first, scale in ((out_eg, 0, edge_scale), (out_ng, 2, node_scale)):
        gain_line = jnp.where(pair == 0, gains[first : first + 1], gains[first + 1 : first + 2])
        out[...] = jnp.where(core == 0, gain_line[:, :quarter], gain_line[:, quarter:]) * scale
    for halo in halos:
        halo.wait()
    owner = lax.broadcasted_iota(jnp.int32, (owned, slots), 0)
    for direction in range(4):
        hot = one_hot(owner == recv_index[direction : direction + 1, :])
        node_part = node_part + matmul(hot, ghost_in[direction])
    stage_across(0)
    grad_node[...] = narrow(node_part)
    for number in (0, 5, 9):
        saves[number].start()
    stage_spread(2)
    stage_across(1)
    stage_out(0, (out_n1, out_n2, out_n3), node_scale)
    for number in (6, 7, 8):
        saves[number].start()
    stage_out(1, (out_e2, out_e3), edge_scale)
    for number in (3, 4):
        saves[number].start()
    stage_out(2, (out_e1,), edge_scale)
    saves[2].start()
    for save in saves:
        save.wait()


def store_kernel(*refs):
    ins, outs, held = refs[:10], refs[10:20], refs[20:30]
    load_sem, store_sem = refs[30:]
    loads = [pltpu.make_async_copy(ins[at], held[at], load_sem.at[at]) for at in range(10)]
    stores = [pltpu.make_async_copy(held[at], outs[at], store_sem.at[at]) for at in range(10)]
    for load in loads:
        load.start()
    for load, store in zip(loads, stores):
        load.wait()
        store.start()
    for store in stores:
        store.wait()


def fused_device(
    node_latents,
    ghost_latents,
    edge_latents,
    node_cotangent,
    edge_cotangent,
    senders,
    receivers,
    halo_counts,
    recv_index,
    edge_w1,
    edge_w2,
    edge_w3,
    edge_gain,
    node_w1,
    node_w2,
    node_w3,
    node_gain,
):
    domains = lax.axis_size("dom")
    groups = lax.axis_size("grp")
    nodes, latent = node_latents.shape[1:]
    edges = edge_latents.shape[1]
    slots = ghost_latents.shape[1] // 4
    partitions = domains * groups
    plan = (
        domains,
        1.0 / math.sqrt(partitions * edges),
        1.0 / math.sqrt(partitions * nodes),
    )
    half = latent // 2
    quarter = latent // 4
    blocks = domains // 2
    bulk = [
        node_w1.shape[0] // 4 + 2 * quarter,
        2 * quarter,
        edge_w1.shape[0] // 4,
    ]
    clean = [rows // blocks for rows in bulk]
    sizes = [clean[0], clean[1] + 16, clean[2]]

    def buffers(lead, kind, rows=sizes):
        return [pltpu.VMEM((*lead, size, half), kind) for size in rows]

    scratch = (
        buffers((2, 2, domains), jnp.bfloat16)
        + buffers((2, domains), jnp.bfloat16)
        + buffers((domains,), jnp.bfloat16)
        + buffers((domains,), jnp.float32)
        + buffers((domains,), jnp.bfloat16)
        + buffers((domains,), jnp.bfloat16)
        + buffers((domains,), jnp.bfloat16)
        + buffers((domains,), jnp.bfloat16, clean)
        + [
            pltpu.VMEM((4, slots, latent), jnp.bfloat16),
            pltpu.VMEM((4, slots, latent), jnp.bfloat16),
        ]
    )
    copies = 3 * (2 + 2 * (domains - 1)) + 4
    scratch += [pltpu.SemaphoreType.DMA((copies,)), pltpu.SemaphoreType.DMA((copies,))]
    operands = (
        node_latents[0],
        ghost_latents[0],
        edge_latents[0],
        node_cotangent[0],
        edge_cotangent[0],
        senders,
        receivers,
        halo_counts,
        recv_index[0],
        edge_w1,
        edge_w2,
        edge_w3,
        edge_gain[None],
        node_w1,
        node_w2,
        node_w3,
        node_gain[None],
    )
    scratch += [pltpu.SemaphoreType.DMA((len(operands),))]
    scratch += [pltpu.VMEM(operand.shape, operand.dtype) for operand in operands]

    def grad(rows):
        return jax.ShapeDtypeStruct((rows, latent), jnp.float32)

    gain = jax.ShapeDtypeStruct((1, quarter), jnp.float32)
    shapes = (
        jax.ShapeDtypeStruct((nodes, latent), jnp.bfloat16),
        jax.ShapeDtypeStruct((edges, latent), jnp.bfloat16),
        grad(edge_w1.shape[0] // 4),
        grad(quarter),
        grad(quarter),
        gain,
        grad(node_w1.shape[0] // 4),
        grad(quarter),
        grad(quarter),
        gain,
    )
    scratch += [pltpu.SemaphoreType.DMA((len(shapes),))]
    scratch += [pltpu.VMEM(out.shape, out.dtype) for out in shapes]
    outs = pl.pallas_call(
        functools.partial(fused_kernel, plan),
        out_shape=shapes,
        in_specs=[pl.BlockSpec(memory_space=pltpu.HBM)] * len(operands),
        out_specs=[pl.BlockSpec(memory_space=pltpu.HBM)] * 10,
        scratch_shapes=scratch,
        compiler_params=pltpu.CompilerParams(
            collective_id=0, has_side_effects=True, vmem_limit_bytes=60 * 1024 * 1024
        ),
    )(*operands)
    outs = pl.pallas_call(
        store_kernel,
        out_shape=tuple(jax.ShapeDtypeStruct(out.shape, out.dtype) for out in outs),
        in_specs=[pl.BlockSpec(memory_space=pltpu.HBM)] * 10,
        out_specs=[pl.BlockSpec(memory_space=pltpu.HBM)] * 10,
        scratch_shapes=[pltpu.VMEM(out.shape, out.dtype) for out in outs]
        + [pltpu.SemaphoreType.DMA((10,)), pltpu.SemaphoreType.DMA((10,))],
        compiler_params=pltpu.CompilerParams(vmem_limit_bytes=60 * 1024 * 1024),
    )(*outs)
    outs = list(outs)
    outs[0] = outs[0][None]
    outs[1] = outs[1][None]
    outs[5] = outs[5][0]
    outs[9] = outs[9][0]
    return tuple(outs)


def solution(mesh):
    placed = (
        P("grp", "dom", None),
        P("grp", "dom", None),
        P("grp", "dom", None),
        P("grp", "dom", None),
        P("grp", "dom", None),
        P("grp", "dom"),
        P("grp", "dom"),
        P("grp", "dom"),
        P("grp", "dom", None),
        P(),
        P(),
        P(),
        P(),
        P(),
        P(),
        P(),
        P(),
    )
    domains, groups = mesh.shape["dom"], mesh.shape["grp"]
    fits = groups == 4 and domains == 8
    return jax.shard_map(
        fused_device if fits else per_device,
        mesh=mesh,
        in_specs=placed,
        out_specs=(
            P("grp", "dom", None),
            P("grp", "dom", None),
            P("grp", None),
            P("grp", None),
            P("grp", None),
            P("grp"),
            P("grp", None),
            P("grp", None),
            P("grp", None),
            P("grp"),
        ),
        check_vma=False,
    )
```
